32 devices in a mesh: fsdp: 16 (over z, y, core), expert: 2 (over x).
Axes of the slice: x: 2, y: 2, z: 4, core: 2. Of those that a mesh axis runs over, the one named last changes fastest.
Arguments:
- tokens: bfloat16 [2048, 5120], P('expert', 'fsdp'), may hold values from -6 to 6
- out_grad: bfloat16 [2048, 5120], P('expert', 'fsdp'), may hold values from -6 to 6
- slot_rows: int32 [2, 2, 24], P('expert'), may hold values from 0 to 1023, as said below
- expert_counts: int32 [2, 2], P('expert'), may hold values from 1 to 24, as said below
- route_prob: float32 [2, 48], P('expert'), may hold values from 0.05 to 0.9
- w_gate: bfloat16 [2, 5120, 1536], P('expert', 'fsdp'), may hold values from -0.078125 to 0.078125
- w_up: bfloat16 [2, 5120, 1536], P('expert', 'fsdp'), may hold values from -0.078125 to 0.078125
- w_down: bfloat16 [2, 5120, 1536], P('expert', 'fsdp'), may hold values from -0.15625 to 0.15625
Outputs:
- token_grad: bfloat16 [2048, 5120], P('expert', 'fsdp')
- gate_grad: float32 [2, 5120, 1536], P('expert', 'fsdp')
- up_grad: float32 [2, 5120, 1536], P('expert', 'fsdp')
- down_grad: float32 [2, 5120, 1536], P('expert', 'fsdp')
- prob_grad: float32 [2, 48], P('expert', 'fsdp')
The draws below stay inside these ranges and needn't reach their ends.
Inputs may be any that keep to these rules, and one draw needn't show every extreme that they name: `slot_rows`: for each token group and expert the 24 listed rows are distinct. `expert_counts`: in every draw one expert has all 24 slots live from every token group.
All inputs are finite; a program needn't handle non-finite values.
Results may differ from the reference program's by a relative error of at most 0.0055.
Values may be sent and summed in bfloat16 or wider, within the bound.
No kernel may reach another device: no remote copies, remote signals or barrier semaphores. Data moves between devices by JAX's collectives and lax.ppermute only.
A program may use at most 64 MiB of HBM per device.

```python
import math
import jax
import jax.numpy as jnp
from jax import lax

D = 5120
FF = 1536
TOK_DEV = 1024
SLOT = 24
SOURCES = 2
EXPERTS = 2
TOKENS = 2048


def draw_slot_rows(key, part):
    keys = jax.random.split(jax.random.fold_in(key, 11), SOURCES * EXPERTS)
    picks = jax.vmap(lambda one_key: jax.random.permutation(one_key, TOK_DEV)[:SLOT])(keys)
    return picks.reshape(SOURCES, EXPERTS, SLOT).astype(jnp.int32)


def draw_expert_counts(key, part):
    hot_key, other_key = jax.random.split(jax.random.fold_in(key, 23))
    hottest = jax.random.randint(hot_key, (), 0, EXPERTS)
    others = jax.random.randint(other_key, (EXPERTS, SOURCES), max(1, SLOT // 8), SLOT // 2 + 1)
    chosen = jnp.arange(EXPERTS)[:, None] == hottest
    return jnp.where(chosen, SLOT, others).astype(jnp.int32)


def block_levels(key, shape, shards, least, largest):
    loudness, own = 1.0, jax.random.fold_in(key, 6)
    for position, shards_of in shards:
        draws = jnp.exp(jax.random.uniform(jax.random.fold_in(own, position), (shards_of,), jnp.float32, least / len(shards), largest / len(shards)))
        loudness = loudness * jnp.repeat(draws, shape[position] // shards_of).reshape([-1 if axis == position else 1 for axis in range(len(shape))])
    return loudness


def centred(key, extent, scale, most, cuts=(), kind=jnp.bfloat16):
    array = scale * jax.random.normal(key, extent, jnp.float32)
    if cuts:
        array = array * block_levels(key, extent, cuts, -0.22, 0.18)
    return jnp.clip(array, -most, most).astype(kind)


def setup_inputs(seed: int = 0) -> dict:
    key_of = jax.random.split(jax.random.key(seed), 9)
    return {
        "tokens": centred(key_of[0], (TOKENS, D), 1.0, 6.0, ((0, 2), (1, 16))),
        "out_grad": centred(key_of[1], (TOKENS, D), 1.0, 6.0, ((0, 2), (1, 16))),
        "slot_rows": draw_slot_rows(jax.random.fold_in(key_of[8], 71), 0),
        "expert_counts": draw_expert_counts(jax.random.fold_in(key_of[8], 71), 0),
        "route_prob": jnp.clip(jnp.exp(math.log(0.9) - 2.8903717 * jax.random.uniform(key_of[4], (EXPERTS, SOURCES * SLOT), jnp.float32) ** block_levels(key_of[4], (EXPERTS, SOURCES * SLOT), ((0, 2),), -0.2, 0.2)), 0.05, 0.9),
        "w_gate": centred(key_of[5], (EXPERTS, D, FF), D ** -0.5, 0.078125, ((0, 2), (1, 16))),
        "w_up": centred(key_of[6], (EXPERTS, D, FF), D ** -0.5, 0.078125, ((0, 2), (1, 16))),
        "w_down": centred(key_of[7], (EXPERTS, D, FF), FF ** -0.5, 0.15625, ((0, 2), (1, 16))),
    }


def hidden_backward(gate_sum, up_sum, down_sum, row_prob, live_mask):
    sigmoid_gate = jax.nn.sigmoid(gate_sum)
    silu_gate = gate_sum * sigmoid_gate
    hidden = lax.optimization_barrier((silu_gate * up_sum).astype(jnp.bfloat16)).astype(jnp.float32)
    row_scale = (row_prob * live_mask)[:, None]
    scaled_hidden = (hidden * row_scale).astype(jnp.bfloat16)
    hidden_grad = down_sum * row_scale
    up_act_grad = (hidden_grad * silu_gate).astype(jnp.bfloat16)
    gate_act_grad = (hidden_grad * up_sum * sigmoid_gate * (1.0 + gate_sum * (1.0 - sigmoid_gate))).astype(jnp.bfloat16)
    prob_grad = live_mask * jnp.sum(hidden * down_sum, axis=1)
    return scaled_hidden, gate_act_grad, up_act_grad, prob_grad


def reference(tokens, out_grad, slot_rows, expert_counts, route_prob, w_gate, w_up, w_down):
    offsets = (jnp.arange(SOURCES, dtype=jnp.int32) * TOK_DEV)[:, None]
    slot_index = jnp.arange(SLOT, dtype=jnp.int32)
    token_grad = jnp.zeros((TOKENS, D), jnp.float32)
    gate_grads = []
    up_grads = []
    down_grads = []
    prob_grads = []
    for expert in range(EXPERTS):
        row_index = (slot_rows[:, expert, :].astype(jnp.int32) + offsets).reshape(-1).astype(jnp.int32)
        token_rows = tokens[row_index]
        grad_rows = out_grad[row_index]
        live_mask = (slot_index[None, :] < expert_counts[expert][:, None]).reshape(-1).astype(jnp.float32)
        gate_sum = jnp.dot(token_rows, w_gate[expert], preferred_element_type=jnp.float32)
        up_sum = jnp.dot(token_rows, w_up[expert], preferred_element_type=jnp.float32)
        down_sum = jnp.dot(grad_rows, w_down[expert], preferred_element_type=jnp.float32)
        scaled_hidden, gate_act_grad, up_act_grad, prob_grad = hidden_backward(gate_sum, up_sum, down_sum, route_prob[expert], live_mask)
        gate_grads.append(jnp.dot(token_rows.T, gate_act_grad, preferred_element_type=jnp.float32))
        up_grads.append(jnp.dot(token_rows.T, up_act_grad, preferred_element_type=jnp.float32))
        down_grads.append(jnp.dot(grad_rows.T, scaled_hidden, preferred_element_type=jnp.float32))
        prob_grads.append(prob_grad)
        slot_grad = (jnp.dot(gate_act_grad, w_gate[expert].T, preferred_element_type=jnp.float32) + jnp.dot(up_act_grad, w_up[expert].T, preferred_element_type=jnp.float32)).astype(jnp.bfloat16)
        token_grad = token_grad.at[row_index].add(slot_grad.astype(jnp.float32))
    return (token_grad.astype(jnp.bfloat16), jnp.stack(gate_grads), jnp.stack(up_grads), jnp.stack(down_grads), jnp.stack(prob_grads))
```

```python
import jax
import jax.numpy as jnp
from jax import lax
from jax.experimental import pallas as pl
from jax.experimental.pallas import tpu as pltpu
from jax.sharding import PartitionSpec as P

BF16 = jnp.bfloat16
F32 = jnp.float32
VMEM = pl.BlockSpec(memory_space=pltpu.VMEM)
SMEM = pl.BlockSpec(memory_space=pltpu.SMEM)
PARAMS = pltpu.CompilerParams(vmem_limit_bytes=40 * 2**20)


def dot(a, b, contract):
    return lax.dot_general(a, b, ((contract[0:1], contract[1:2]), ((), ())), preferred_element_type=F32)


def gather_kernel(order, slot_rows, tokens_t, grads_t, rows_out, onehot_out, onehot_f):
    experts, slots = slot_rows.shape
    count = tokens_t.shape[1]
    lane = lax.broadcasted_iota(jnp.int32, (8, count), 1)
    sub = lax.broadcasted_iota(jnp.int32, (8, count), 0)
    for j in range(experts):
        for base in range(0, slots, 8):
            picked = jnp.zeros((8, count), jnp.int32)
            for r in range(8):
                picked = jnp.where(sub == r, slot_rows[order[j], base + r], picked)
            onehot_f[pl.ds(j * slots + base, 8), :] = (picked == lane).astype(F32)
    onehot = onehot_f[...].astype(BF16)
    onehot_out[...] = onehot
    for kind, source in enumerate((tokens_t, grads_t)):
        rows = dot(onehot, source[...], (1, 1))
        for j in range(experts):
            rows_out[j, kind] = rows[j * slots : (j + 1) * slots].astype(BF16)


def stacked_rows(blocks, kind):
    return jnp.concatenate([block[kind].astype(F32) for block in blocks], axis=0).astype(BF16)


def partial_kernel(where, own, recv, w_gate, w_up, w_down, out):
    blocks = [own] + [recv.at[j] for j in range(recv.shape[0])]
    tok, grad = stacked_rows(blocks, 0), stacked_rows(blocks, 1)
    chunk_rows, width = out.shape[1] // 3, out.shape[2]
    for jy in range(2):
        column = where[0] + ((where[1] & 1) ^ jy) * width
        at = pl.ds(pl.multiple_of(column, 128), width)
        for q, (x, w) in enumerate(((tok, w_gate), (tok, w_up), (grad, w_down))):
            sums = dot(x, w[0, :, at], (1, 0))
            for part in range(2):
                chunk = ((where[1] >> 1) ^ part) * 2 + jy
                out[chunk, pl.ds(q * chunk_rows, chunk_rows), :] = sums[part * chunk_rows : (part + 1) * chunk_rows]


def hidden_kernel(order, part, counts, prob, sums, recv, out):
    experts = counts.shape[0]
    slots = prob.shape[1] // experts
    total_rows = prob.shape[1]
    rows = sums.shape[0] // 3
    padded = out.shape[0] // 3
    width = sums.shape[1]
    total = sums[...] + recv[...]
    gate, up, down = total[:rows], total[rows : 2 * rows], total[2 * rows :]
    row = lax.broadcasted_iota(jnp.int32, (rows, 1), 0) + part[0] * rows
    slot = row
    place = jnp.zeros((rows, 1), jnp.int32)
    live_count = jnp.zeros((rows, 1), jnp.int32)
    for j in range(experts):
        inside = (row >= j * slots) & (row < (j + 1) * slots)
        slot = jnp.where(inside, row - j * slots, slot)
        place = jnp.where(inside, order[j] * slots + row - j * slots, place)
        live_count = jnp.where(inside, counts[order[j]], live_count)
    live = (slot < live_count).astype(F32)
    diagonal = lax.broadcasted_iota(jnp.int32, (rows, total_rows), 1) == place
    row_prob = jnp.sum(jnp.where(diagonal, prob[...], 0.0), axis=1, keepdims=True)
    scale = row_prob * live
    sigmoid = jax.nn.sigmoid(gate)
    silu = gate * sigmoid
    hidden = (silu * up).astype(BF16).astype(F32)
    hidden_grad = down * scale
    prob_grad = live * jnp.sum(hidden * down, axis=1, keepdims=True)
    prob_row = jnp.sum(jnp.where(diagonal, prob_grad, 0.0), axis=0, keepdims=True)
    high = prob_row.astype(BF16).astype(F32)
    tail = jnp.concatenate([high, prob_row - high, jnp.zeros((padded - rows - 2, total_rows), F32)], axis=0)
    tail = jnp.concatenate([tail, jnp.zeros((padded - rows, width - total_rows), F32)], axis=1)
    zeros = jnp.zeros((padded - rows, width), F32)
    gate_act_grad = hidden_grad * up * sigmoid * (1.0 + gate * (1.0 - sigmoid))
    for q, (x, end) in enumerate(((hidden * scale, tail), (gate_act_grad, zeros), (hidden_grad * silu, zeros))):
        out[pl.ds(q * padded, padded), :] = jnp.concatenate([x, end], axis=0).astype(BF16)


def piece(near, far, where, side, jy, q, rows):
    acts = far if side else near
    padded = acts.shape[1] // 3
    at = pl.ds(q * padded, padded)
    halves = [acts[((where[1] >> 1) ^ part) * 2 + jy, at, :].astype(F32)[: rows // 2] for part in range(2)]
    return jnp.concatenate(halves, axis=0).astype(BF16)


def piece_column(where, side, jy, width):
    base = where[0] if side == 0 else 2 * width - where[0]
    return base + ((where[1] & 1) ^ jy) * width


def slot_kernel(where, near, far, w_gate, w_up, out, prob_out):
    width = near.shape[2]
    slots = out.shape[1]
    rows = out.shape[0] * slots
    padded = near.shape[1] // 3
    total = jnp.zeros((rows, out.shape[2]), F32)
    tail = jnp.zeros((padded - rows // 2, width), F32)
    for side in range(2):
        for jy in range(2):
            at = pl.ds(pl.multiple_of(piece_column(where, side, jy, width), 128), width)
            for q, w in ((1, w_gate), (2, w_up)):
                total += dot(piece(near, far, where, side, jy, q, rows), w[0, :, at], (1, 1))
            for jz in range(2):
                acts = far if side else near
                tail += acts[jz * 2 + jy, pl.ds(0, padded), :].astype(F32)[rows // 2 :]
    for j in range(out.shape[0]):
        out[j] = total[j * slots : (j + 1) * slots].astype(BF16)
    prob_out[...] = tail[0:1] + tail[1:2]


def weight_grad_kernel(where, own, recv, near, far, gate_grad, up_grad, down_grad):
    blocks = [own] + [recv.at[j] for j in range(recv.shape[0])]
    tok, grad = stacked_rows(blocks, 0), stacked_rows(blocks, 1)
    rows = tok.shape[0]
    for i in range(4):
        @pl.when(pl.program_id(0) == i)
        def _(i=i):
            side, jy = i // 2, i % 2
            for q, x, out in ((0, grad, down_grad), (1, tok, gate_grad), (2, tok, up_grad)):
                out[0] = dot(x, piece(near, far, where, side, jy, q, rows), (0, 0))


def token_grad_kernel(own, recv, onehot, out):
    blocks = [own[...]] + [recv[j] for j in range(recv.shape[0])]
    slot_grad = jnp.concatenate([block.astype(F32) for block in blocks], axis=0).astype(BF16)
    out[...] = dot(slot_grad, onehot[...], (0, 0)).astype(BF16)


def local(tokens, out_grad, slot_rows, expert_counts, route_prob, w_gate, w_up, w_down):
    fsdp, experts = lax.axis_size("fsdp"), lax.axis_size("expert")
    steps = fsdp.bit_length() - 1
    me, my_expert = lax.axis_index("fsdp"), lax.axis_index("expert")
    token_count, features = tokens.shape
    _, _, slots = slot_rows.shape
    rows = experts * slots
    hidden = w_gate.shape[2]
    half, quarter = hidden // 2, hidden // 4
    side, corner = me & 1, (me >> 1) & 3
    where = jnp.stack([side * half, corner]).astype(jnp.int32)
    other = jnp.stack([(1 - side) * half, corner]).astype(jnp.int32)

    def swap(x, mask):
        return lax.ppermute(x, "fsdp", [(i, i ^ mask) for i in range(fsdp)])

    def to_expert(x):
        if experts == 2:
            return x[0], lax.ppermute(x[1], "expert", [(0, 1), (1, 0)])[None]
        moved = lax.all_to_all(x, "expert", split_axis=0, concat_axis=0, tiled=True)
        return moved[0], moved[1:]

    if experts == 2:
        order = jnp.stack([my_expert, 1 - my_expert]).astype(jnp.int32)
    else:
        order = jnp.arange(experts, dtype=jnp.int32)

    rows_out, onehot = pl.pallas_call(
        gather_kernel,
        out_shape=(
            jax.ShapeDtypeStruct((experts, 2, slots, features), BF16),
            jax.ShapeDtypeStruct((rows, token_count), BF16),
        ),
        in_specs=[SMEM, SMEM, VMEM, VMEM],
        out_specs=(VMEM, VMEM),
        scratch_shapes=[pltpu.VMEM((rows, token_count), F32)],
        compiler_params=PARAMS,
        name="gather_rows",
    )(order, slot_rows[0], tokens.T, out_grad.T)
    own, recv = to_expert(rows_out)

    def partial(which):
        return pl.pallas_call(
            partial_kernel,
            out_shape=jax.ShapeDtypeStruct((4, 3 * rows // 2, quarter), F32),
            in_specs=[SMEM] + [VMEM] * 5,
            out_specs=VMEM,
            compiler_params=PARAMS,
            cost_estimate=pl.CostEstimate(
                flops=6 * rows * features * half, bytes_accessed=3 * features * half * 2, transcendentals=0
            ),
            name="partial_sums",
        )(which, own, recv, w_gate, w_up, w_down)

    sent = partial(other)
    arrived = swap(sent, 1)
    kept = partial(where)
    total = kept + arrived
    total = total[0] + swap(total[1], 2) + swap(total[2], 4) + swap(total[3], 6)
    for b in range(3, steps):
        arrived = swap(total, 1 << b)
        if b < steps - 1:
            total = total + arrived
    padded = (rows // 2 + 2 + 15) // 16 * 16
    acts = pl.pallas_call(
        hidden_kernel,
        out_shape=jax.ShapeDtypeStruct((3 * padded, quarter), BF16),
        in_specs=[SMEM, SMEM, SMEM, VMEM, VMEM, VMEM],
        out_specs=VMEM,
        compiler_params=PARAMS,
        name="hidden",
    )(order, (corner >> 1)[None], expert_counts[0], route_prob, total, arrived)
    near = jnp.stack([acts, swap(acts, 2), swap(acts, 4), swap(acts, 6)])
    far = swap(near, 1)

    slot_grad, prob_row = pl.pallas_call(
        slot_kernel,
        out_shape=(
            jax.ShapeDtypeStruct((experts, slots, features), BF16),
            jax.ShapeDtypeStruct((1, quarter), F32),
        ),
        in_specs=[SMEM, VMEM, VMEM, VMEM, VMEM],
        out_specs=(VMEM, VMEM),
        compiler_params=PARAMS,
        name="slot_grad",
    )(where, near, far, w_gate, w_up)
    slot_own, slot_recv = to_expert(slot_grad)

    grad_shape = jax.ShapeDtypeStruct((1, features, hidden), F32)

    def grad_place(i, where):
        base = jnp.where(i < 2, where[0], half - where[0]) // quarter
        return 0, 0, base + ((where[1] & 1) ^ (i & 1))

    grad_spec = pl.BlockSpec((1, features, quarter), grad_place)
    whole = lambda x: pl.BlockSpec(x.shape, lambda i, where: (0,) * x.ndim)
    gate_grad, up_grad, down_grad = pl.pallas_call(
        weight_grad_kernel,
        out_shape=(grad_shape,) * 3,
        grid_spec=pltpu.PrefetchScalarGridSpec(
            num_scalar_prefetch=1,
            grid=(4,),
            in_specs=[whole(x) for x in (own, recv, near, far)],
            out_specs=(grad_spec,) * 3,
        ),
        compiler_params=PARAMS,
        cost_estimate=pl.CostEstimate(
            flops=6 * rows * features * hidden, bytes_accessed=12 * features * hidden, transcendentals=0
        ),
        name="weight_grads",
    )(where, own, recv, near, far)

    token_grad = pl.pallas_call(
        token_grad_kernel,
        out_shape=jax.ShapeDtypeStruct((features, token_count), BF16),
        in_specs=[VMEM] * 3,
        out_specs=VMEM,
        compiler_params=PARAMS,
        name="token_grad",
    )(slot_own, slot_recv, onehot).T
    share = rows // fsdp
    prob_grad = lax.dynamic_slice_in_dim(prob_row, me * share, share, axis=1)
    return (token_grad, gate_grad, up_grad, down_grad, prob_grad)


def solution(mesh):
    return jax.shard_map(
        local,
        mesh=mesh,
        in_specs=(
            P("expert", "fsdp"),
            P("expert", "fsdp"),
            P("expert", None, None),
            P("expert", None),
            P("expert", None),
            P("expert", "fsdp", None),
            P("expert", "fsdp", None),
            P("expert", "fsdp", None),
        ),
        out_specs=(
            P("expert", "fsdp"),
            P("expert", "fsdp", None),
            P("expert", "fsdp", None),
            P("expert", "fsdp", None),
            P("expert", "fsdp"),
        ),
        check_vma=False,
    )
```

```python
import functools

import jax
import jax.numpy as jnp
from jax import lax
from jax.experimental import pallas as pl
from jax.experimental.pallas import tpu as pltpu
from jax.sharding import PartitionSpec as P

BF16 = jnp.bfloat16
F32 = jnp.float32
VMEM = pl.BlockSpec(memory_space=pltpu.VMEM)
HBM = pl.BlockSpec(memory_space=pltpu.HBM)
SMEM = pl.BlockSpec(memory_space=pltpu.SMEM)
PARAMS = pltpu.CompilerParams(vmem_limit_bytes=40 * 2**20)


def in_hbm(x):
    return pltpu.with_memory_space_constraint(x, pltpu.HBM)


def dot(a, b, contract):
    return lax.dot_general(a, b, ((contract[0:1], contract[1:2]), ((), ())), preferred_element_type=F32)


def place(side, jy, width):
    me = lax.axis_index("fsdp")
    half = (me & 1) ^ side
    return pl.multiple_of((half * 2 + (((me >> 1) & 1) ^ jy)) * width, 128)


def row_part():
    return (lax.axis_index("fsdp") >> 2) & 1


def first_expert(experts):
    return lax.axis_index("expert") if experts == 2 else 0


def gather_kernel(slot_rows_hbm, tokens_hbm, grads_hbm, rows_out, onehot_out, slot_rows, tokens_t, grads_t, onehot_f, sems):
    copies = [
        pltpu.make_async_copy(source, to, sems.at[i])
        for i, (source, to) in enumerate(((slot_rows_hbm, slot_rows), (tokens_hbm, tokens_t), (grads_hbm, grads_t)))
    ]
    for copy in copies:
        copy.start()
    experts, slots = slot_rows.shape
    count = tokens_t.shape[1]
    first = first_expert(experts)
    lane = lax.broadcasted_iota(jnp.int32, (8, count), 1)
    sub = lax.broadcasted_iota(jnp.int32, (8, count), 0)
    copies[0].wait()
    for j in range(experts):
        expert = lax.rem(first + j, experts)
        for base in range(0, slots, 8):
            picked = jnp.zeros((8, count), jnp.int32)
            for r in range(8):
                picked = jnp.where(sub == r, slot_rows[expert, base + r], picked)
            onehot_f[pl.ds(j * slots + base, 8), :] = (picked == lane).astype(F32)
    onehot = onehot_f[...].astype(BF16)
    onehot_out[...] = onehot
    for kind, source in enumerate((tokens_t, grads_t)):
        copies[1 + kind].wait()
        rows = dot(onehot, source[...], (1, 1))
        for j in range(experts):
            rows_out[j, kind] = rows[j * slots : (j + 1) * slots].astype(BF16)


def load_kernel(after, w_gate, w_up, w_down, gate_out, up_out, down_out, sems):
    del after
    copies = [
        pltpu.make_async_copy(w.at[0], to, sems.at[i])
        for i, (w, to) in enumerate(((w_gate, gate_out), (w_up, up_out), (w_down, down_out)))
    ]
    for copy in copies:
        copy.start()
    for copy in copies:
        copy.wait()


def stacked_rows(own, recv, kind):
    blocks = [own[kind]] + [recv[j, kind] for j in range(recv.shape[0])]
    return jnp.concatenate([block.astype(F32) for block in blocks], axis=0)


def partial_kernel(side, own, recv, w_gate, w_up, w_down, out, *turned):
    tok, grad = stacked_rows(own, recv, 0), stacked_rows(own, recv, 1)
    chunk_rows, width = out.shape[1] // 3, out.shape[2]
    part0 = row_part()
    for to, x in zip(turned, (tok, grad)):
        padded = to.shape[1] // 2
        zeros = jnp.zeros((padded - chunk_rows, x.shape[1]), F32)
        low, high = x[:chunk_rows], x[chunk_rows:]
        near, far = jnp.where(part0 == 0, low, high), jnp.where(part0 == 0, high, low)
        to[...] = jnp.concatenate([near, zeros, far, zeros], axis=0).T.astype(BF16)
    tok, grad = tok.astype(BF16), grad.astype(BF16)
    for jy in range(2):
        at = pl.ds(place(side, jy, width), width)
        for q, (x, w) in enumerate(((tok, w_gate), (tok, w_up), (grad, w_down))):
            sums = dot(x, w[:, at], (1, 0))
            for part in range(2):
                chunk = (part0 ^ part) * 2 + jy
                out[chunk, pl.ds(q * chunk_rows, chunk_rows), :] = sums[part * chunk_rows : (part + 1) * chunk_rows]


def add_kernel(kept, arrived, *outs):
    for j, out in enumerate(outs):
        out[...] = kept[j] + arrived[j]


def hidden_kernel(counts, prob, sums, recv, out):
    experts = counts.shape[0]
    slots = prob.shape[1] // experts
    total_rows = prob.shape[1]
    rows = sums.shape[0] // 3
    padded = out.shape[0] // 3
    width = sums.shape[1]
    total = sums[...] + recv[...]
    gate, up, down = total[:rows], total[rows : 2 * rows], total[2 * rows :]
    row = lax.broadcasted_iota(jnp.int32, (rows, 1), 0) + row_part() * rows
    slot = row
    home = jnp.zeros((rows, 1), jnp.int32)
    first = first_expert(experts)
    live_count = jnp.zeros((rows, 1), jnp.int32)
    for j in range(experts):
        inside = (row >= j * slots) & (row < (j + 1) * slots)
        slot = jnp.where(inside, row - j * slots, slot)
        source = lax.rem(first + j, experts)
        home = jnp.where(inside, source * slots + row - j * slots, home)
        live_count = jnp.where(inside, counts[source], live_count)
    live = (slot < live_count).astype(F32)
    diagonal = lax.broadcasted_iota(jnp.int32, (rows, total_rows), 1) == home
    row_prob = jnp.sum(jnp.where(diagonal, prob[...], 0.0), axis=1, keepdims=True)
    scale = row_prob * live
    sigmoid = jax.nn.sigmoid(gate)
    silu = gate * sigmoid
    hidden = (silu * up).astype(BF16).astype(F32)
    hidden_grad = down * scale
    prob_grad = live * jnp.sum(hidden * down, axis=1, keepdims=True)
    prob_row = jnp.sum(jnp.where(diagonal, prob_grad, 0.0), axis=0, keepdims=True)
    high = prob_row.astype(BF16).astype(F32)
    tail = jnp.concatenate([high, prob_row - high, jnp.zeros((padded - rows - 2, total_rows), F32)], axis=0)
    tail = jnp.concatenate([tail, jnp.zeros((padded - rows, width - total_rows), F32)], axis=1)
    zeros = jnp.zeros((padded - rows, width), F32)
    gate_act_grad = hidden_grad * up * sigmoid * (1.0 + gate * (1.0 - sigmoid))
    for q, (x, end) in enumerate(((hidden * scale, tail), (gate_act_grad, zeros), (hidden_grad * silu, zeros))):
        out[pl.ds(q * padded, padded), :] = jnp.concatenate([x, end], axis=0).astype(BF16)


def both_parts(a, b, q):
    padded = a.shape[0] // 3
    return jnp.concatenate([a[pl.ds(q * padded, padded), :], b[pl.ds(q * padded, padded), :]], axis=0)


def slot_part(a, b, w_gate, w_up, column):
    at = pl.ds(column, a.shape[1])
    return dot(both_parts(a, b, 1), w_gate[:, at], (1, 1)) + dot(both_parts(a, b, 2), w_up[:, at], (1, 1))


def near_slot_kernel(near0, near1, near2, near3, w_gate, w_up, out):
    width = near0.shape[1]
    out[...] = slot_part(near0, near2, w_gate, w_up, place(0, 0, width)) + slot_part(
        near1, near3, w_gate, w_up, place(0, 1, width)
    )


def slot_kernel(before, far, w_gate, w_up, out):
    width = far.shape[2]
    padded = far.shape[1] // 3
    experts, slots, _ = out.shape
    total = before[...]
    for jy in range(2):
        total += slot_part(far.at[jy], far.at[2 + jy], w_gate, w_up, place(1, jy, width))
    for part in range(2):
        for j in range(experts // 2):
            start = part * padded + j * slots
            out[(row_part() ^ part) * (experts // 2) + j] = total[start : start + slots].astype(BF16)


def weight_grad_kernel(chunk_rows, near0, near1, near2, near3, far, tok_t, grad_t, gate_grad, up_grad, down_grad, prob_out, held, sems):
    width = far.shape[2]
    padded = far.shape[1] // 3
    pieces = [(near0, near2), (near1, near3), (far.at[0], far.at[2]), (far.at[1], far.at[3])]
    copies = []
    for i, (a, b) in enumerate(pieces):
        for q, x, out in ((0, grad_t, down_grad), (1, tok_t, gate_grad), (2, tok_t, up_grad)):
            n = len(copies)
            held[n] = dot(x[...], both_parts(a, b, q), (1, 0))
            to = out.at[0, :, pl.ds(place(i // 2, i % 2, width), width)]
            copy = pltpu.make_async_copy(held.at[n], to, sems.at[n])
            copy.start()
            copies.append(copy)
    tail = jnp.zeros((16, width), F32)
    for a, b in pieces:
        tail += a[pl.ds(padded - 16, 16), :].astype(F32) + b[pl.ds(padded - 16, 16), :].astype(F32)
    start = 16 - (padded - chunk_rows)
    prob = jnp.broadcast_to(tail[start : start + 1] + tail[start + 1 : start + 2], (8, width))
    share = prob_out.shape[1]
    shift = lax.rem(width - lax.axis_index("fsdp") * share, width)
    prob_out[...] = pltpu.roll(prob, shift, 1)[:1, :share]
    for copy in copies:
        copy.wait()


def token_grad_kernel(own, recv, onehot, out):
    blocks = [own[...]] + [recv[j] for j in range(recv.shape[0])]
    slot_grad = jnp.concatenate([block.astype(F32) for block in blocks], axis=0).astype(BF16)
    out[...] = dot(slot_grad, onehot[...], (0, 0)).astype(BF16)


def local(tokens, out_grad, slot_rows, expert_counts, route_prob, w_gate, w_up, w_down):
    fsdp, experts = lax.axis_size("fsdp"), lax.axis_size("expert")
    steps = fsdp.bit_length() - 1
    token_count, features = tokens.shape
    _, _, slots = slot_rows.shape
    rows = experts * slots
    hidden = w_gate.shape[2]
    half, quarter = hidden // 2, hidden // 4
    def swap(x, mask):
        return lax.ppermute(x, "fsdp", [(i, i ^ mask) for i in range(fsdp)])

    def to_expert(x):
        if experts == 2:
            return x[0], lax.ppermute(x[1], "expert", [(0, 1), (1, 0)])[None]
        moved = lax.all_to_all(x, "expert", split_axis=0, concat_axis=0, tiled=True)
        return moved[0], moved[1:]

    rows_out, onehot = pl.pallas_call(
        gather_kernel,
        out_shape=(
            jax.ShapeDtypeStruct((experts, 2, slots, features), BF16),
            jax.ShapeDtypeStruct((rows, token_count), BF16),
        ),
        in_specs=[HBM] * 3,
        out_specs=(VMEM, VMEM),
        scratch_shapes=[
            pltpu.SMEM((experts, slots), jnp.int32),
            pltpu.VMEM((features, token_count), BF16),
            pltpu.VMEM((features, token_count), BF16),
            pltpu.VMEM((rows, token_count), F32),
            pltpu.SemaphoreType.DMA((3,)),
        ],
        compiler_params=PARAMS,
        name="gather_rows",
    )(*(in_hbm(x) for x in (slot_rows[0], tokens.T, out_grad.T)))
    own, recv = to_expert(rows_out)
    weights = pl.pallas_call(
        load_kernel,
        out_shape=(jax.ShapeDtypeStruct((features, hidden), BF16),) * 3,
        in_specs=[VMEM] + [HBM] * 3,
        out_specs=(VMEM,) * 3,
        scratch_shapes=[pltpu.SemaphoreType.DMA((3,))],
        compiler_params=PARAMS,
        cost_estimate=pl.CostEstimate(flops=0, bytes_accessed=6 * features * hidden, transcendentals=0),
        name="load_weights",
    )(own, *(in_hbm(w) for w in (w_gate, w_up, w_down)))
    padded = (rows // 2 + 2 + 15) // 16 * 16

    def partial(side, turned):
        turned_shape = jax.ShapeDtypeStruct((features, 2 * padded), BF16)
        shapes = (jax.ShapeDtypeStruct((4, 3 * rows // 2, quarter), F32),) + (turned_shape,) * turned
        return pl.pallas_call(
            functools.partial(partial_kernel, side),
            out_shape=shapes,
            in_specs=[VMEM] * 5,
            out_specs=(VMEM,) * len(shapes),
            compiler_params=PARAMS,
            cost_estimate=pl.CostEstimate(
                flops=6 * rows * features * half, bytes_accessed=3 * features * half * 2, transcendentals=0
            ),
            name="partial_sums",
        )(own, recv, *weights)

    arrived = swap(partial(1, 0)[0], 1)
    kept, tok_t, grad_t = partial(0, 2)
    chunk_shape = jax.ShapeDtypeStruct((3 * rows // 2, quarter), F32)
    chunks = pl.pallas_call(
        add_kernel,
        out_shape=(chunk_shape,) * 4,
        in_specs=[VMEM] * 2,
        out_specs=(VMEM,) * 4,
        compiler_params=PARAMS,
        name="add",
    )(kept, arrived)
    total = chunks[0] + swap(chunks[1], 2) + swap(chunks[2], 4) + swap(chunks[3], 6)
    for b in range(3, steps):
        arrived = swap(total, 1 << b)
        if b < steps - 1:
            total = total + arrived
    acts = pl.pallas_call(
        hidden_kernel,
        out_shape=jax.ShapeDtypeStruct((3 * padded, quarter), BF16),
        in_specs=[SMEM, VMEM, VMEM, VMEM],
        out_specs=VMEM,
        compiler_params=PARAMS,
        name="hidden",
    )(expert_counts[0], route_prob, total, arrived)
    near = [acts, swap(acts, 2), swap(acts, 4), swap(acts, 6)]
    far = swap(jnp.stack(near), 1)

    near_slot = pl.pallas_call(
        near_slot_kernel,
        out_shape=jax.ShapeDtypeStruct((2 * padded, features), F32),
        in_specs=[VMEM] * 6,
        out_specs=VMEM,
        compiler_params=PARAMS,
        cost_estimate=pl.CostEstimate(
            flops=2 * rows * features * hidden, bytes_accessed=2 * features * hidden, transcendentals=0
        ),
        name="near_slot",
    )(*near, weights[0], weights[1])
    slot_grad = pl.pallas_call(
        slot_kernel,
        out_shape=jax.ShapeDtypeStruct((experts, slots, features), BF16),
        in_specs=[VMEM] * 4,
        out_specs=VMEM,
        compiler_params=PARAMS,
        name="slot_grad",
    )(near_slot, far, weights[0], weights[1])
    slot_own, slot_recv = to_expert(slot_grad)
    grad_shape = jax.ShapeDtypeStruct((1, features, hidden), F32)
    gate_grad, up_grad, down_grad, prob_grad = pl.pallas_call(
        functools.partial(weight_grad_kernel, rows // 2),
        out_shape=(grad_shape,) * 3 + (jax.ShapeDtypeStruct((1, rows // fsdp), F32),),
        in_specs=[VMEM] * 7,
        out_specs=(HBM,) * 3 + (VMEM,),
        scratch_shapes=[pltpu.VMEM((12, features, quarter), F32), pltpu.SemaphoreType.DMA((12,))],
        compiler_params=PARAMS,
        cost_estimate=pl.CostEstimate(
            flops=6 * rows * features * hidden, bytes_accessed=12 * features * hidden, transcendentals=0
        ),
        name="weight_grads",
    )(*near, far, tok_t, grad_t)

    token_grad = pl.pallas_call(
        token_grad_kernel,
        out_shape=jax.ShapeDtypeStruct((features, token_count), BF16),
        in_specs=[VMEM] * 3,
        out_specs=VMEM,
        compiler_params=PARAMS,
        name="token_grad",
    )(slot_own, slot_recv, onehot).T
    return (token_grad, gate_grad, up_grad, down_grad, prob_grad)


def solution(mesh):
    return jax.shard_map(
        local,
        mesh=mesh,
        in_specs=(
            P("expert", "fsdp"),
            P("expert", "fsdp"),
            P("expert", None, None),
            P("expert", None),
            P("expert", None),
            P("expert", "fsdp", None),
            P("expert", "fsdp", None),
            P("expert", "fsdp", None),
        ),
        out_specs=(
            P("expert", "fsdp"),
            P("expert", "fsdp", None),
            P("expert", "fsdp", None),
            P("expert", "fsdp", None),
            P("expert", "fsdp"),
        ),
        check_vma=False,
    )
```

```python
import functools

import jax
import jax.numpy as jnp
from jax import lax
from jax.experimental import pallas as pl
from jax.experimental.pallas import tpu as pltpu
from jax.sharding import PartitionSpec as P

BF16 = jnp.bfloat16
F32 = jnp.float32
F16 = jnp.float16
VMEM = pl.BlockSpec(memory_space=pltpu.VMEM)
HBM = pl.BlockSpec(memory_space=pltpu.HBM)
SMEM = pl.BlockSpec(memory_space=pltpu.SMEM)
PARAMS = pltpu.CompilerParams(vmem_limit_bytes=40 * 2**20)

def in_hbm(x):
    return pltpu.with_memory_space_constraint(x, pltpu.HBM)


def dot(a, b, contract):
    return lax.dot_general(a, b, ((contract[0:1], contract[1:2]), ((), ())), preferred_element_type=F32)


def place(side, jy, width):
    me = lax.axis_index("fsdp")
    half = (me & 1) ^ side
    return pl.multiple_of((half * 2 + (((me >> 1) & 1) ^ jy)) * width, 128)


def row_part():
    return (lax.axis_index("fsdp") >> 2) & 1


def first_expert(experts):
    return lax.axis_index("expert") if experts == 2 else 0


def gather_kernel(slot_rows_hbm, tokens_hbm, grads_hbm, rows_out, onehot_out, slot_rows, tokens_t, grads_t, onehot_f, sems):
    copies = [
        pltpu.make_async_copy(source, to, sems.at[i])
        for i, (source, to) in enumerate(((slot_rows_hbm, slot_rows), (tokens_hbm, tokens_t), (grads_hbm, grads_t)))
    ]
    for copy in copies:
        copy.start()
    experts, slots = slot_rows.shape
    count = tokens_t.shape[1]
    first = first_expert(experts)
    lane = lax.broadcasted_iota(jnp.int32, (8, count), 1)
    sub = lax.broadcasted_iota(jnp.int32, (8, count), 0)
    copies[0].wait()
    for j in range(experts):
        expert = lax.rem(first + j, experts)
        for base in range(0, slots, 8):
            picked = jnp.zeros((8, count), jnp.int32)
            for r in range(8):
                picked = jnp.where(sub == r, slot_rows[expert, base + r], picked)
            onehot_f[pl.ds(j * slots + base, 8), :] = (picked == lane).astype(F32)
    onehot = onehot_f[...].astype(BF16)
    onehot_out[...] = onehot
    for kind, source in enumerate((tokens_t, grads_t)):
        copies[1 + kind].wait()
        rows = dot(onehot, source[...], (1, 1))
        for j in range(experts):
            rows_out[j, kind] = rows[j * slots : (j + 1) * slots].astype(BF16)


def load_kernel(after, w_gate, w_up, w_down, gate_out, up_out, down_out, sems):
    del after
    copies = [
        pltpu.make_async_copy(w.at[0], to, sems.at[i])
        for i, (w, to) in enumerate(((w_gate, gate_out), (w_up, up_out), (w_down, down_out)))
    ]
    for copy in copies:
        copy.start()
    for copy in copies:
        copy.wait()


def stacked_rows(own, recv, kind):
    blocks = [own[kind]] + [recv[j, kind] for j in range(recv.shape[0])]
    return jnp.concatenate([block.astype(F32) for block in blocks], axis=0)


def partial_kernel(side, own, recv, w_gate, w_up, w_down, out):
    tok, grad = stacked_rows(own, recv, 0).astype(BF16), stacked_rows(own, recv, 1).astype(BF16)
    chunk_rows, width = out.shape[1] // 3, out.shape[2]
    for jy in range(2):
        at = pl.ds(place(side, jy, width), width)
        for q, (x, w) in enumerate(((tok, w_gate), (tok, w_up), (grad, w_down))):
            sums = dot(x, w[:, at], (1, 0))
            for part in range(2):
                chunk = (row_part() ^ part) * 2 + jy
                out[chunk, pl.ds(q * chunk_rows, chunk_rows), :] = sums[part * chunk_rows : (part + 1) * chunk_rows]


def rows_kernel(counts, own, recv, prob, tok_t, grad_t, scale_out, live_out, diagonal_out):
    part0 = row_part()
    rows, lanes = diagonal_out.shape
    for to, x in ((tok_t, stacked_rows(own, recv, 0)), (grad_t, stacked_rows(own, recv, 1))):
        low, high = x[:rows], x[rows:]
        near, far = jnp.where(part0 == 0, low, high), jnp.where(part0 == 0, high, low)
        to[...] = jnp.concatenate([near, far], axis=0).T.astype(BF16)
    experts = counts.shape[0]
    slots = 2 * rows // experts
    first = first_expert(experts)
    row = lax.broadcasted_iota(jnp.int32, (rows, lanes), 0) + part0 * rows
    lane = lax.broadcasted_iota(jnp.int32, (rows, lanes), 1)
    slot, home, live_count = row, row, row
    for j in range(experts):
        source = lax.rem(first + j, experts)
        inside = (row >= j * slots) & (row < (j + 1) * slots)
        slot = jnp.where(inside, row - j * slots, slot)
        home = jnp.where(inside, source * slots + row - j * slots, home)
        live_count = jnp.where(inside, counts[source], live_count)
    live = (slot < live_count).astype(F32)
    diagonal = lane == home
    probs = jnp.concatenate([prob[...], jnp.zeros((1, lanes - 2 * rows), F32)], axis=1)
    row_prob = jnp.sum(jnp.where(diagonal, probs, 0.0), axis=1, keepdims=True)
    scale_out[...] = row_prob * live[:, :128]
    live_out[...] = live[:, :128]
    diagonal_out[...] = diagonal.astype(F32)


def add_kernel(kept, arrived, first, power_out, *outs):
    rows = first.shape[0] // 3
    width = first.shape[1]
    chunks = [kept[j] + arrived[j] for j in range(4)]
    first[...] = chunks[0]
    powers = []
    for q in range(3):
        most = functools.reduce(jnp.maximum, [jnp.abs(x[q * rows : (q + 1) * rows]) for x in chunks])
        most = jnp.max(jnp.max(most, axis=0, keepdims=True), axis=1, keepdims=True)
        most = jnp.maximum(jnp.broadcast_to(most, (1, width)), 1e-30)
        powers.append(jnp.ceil(jnp.log2(most)) - 14.0)
    power_out[...] = jnp.concatenate(powers + [jnp.zeros((5, width), F32)], axis=0)
    for x, out in zip(chunks[1:], outs):
        for q in range(3):
            out[pl.ds(q * rows, rows), :] = x[q * rows : (q + 1) * rows] * jnp.exp2(-powers[q])
        out[pl.ds(3 * rows, 8), :] = power_out[...]


def scaled(x, power):
    rows = x.shape[0] // 3
    return (x.reshape(3, rows, -1) * jnp.exp2(power[:3])[:, None]).reshape(x.shape)


def coded(x, power):
    return jnp.concatenate([scaled(x, -power), power], axis=0)


def decoded(x):
    x = x.astype(F32)
    return scaled(x[:-8], x[-8:]), x[-8:]


def hidden_kernel(scale, live, diagonal, sums, recv, out):
    rows = sums.shape[0] // 3
    width = sums.shape[1]
    total = sums[...] + recv[...]
    gate, up, down = total[:rows], total[rows : 2 * rows], total[2 * rows :]
    row_scale = jnp.concatenate([scale[...]] * (width // 128), axis=1)
    sigmoid = jax.nn.sigmoid(gate)
    silu = gate * sigmoid
    hidden = (silu * up).astype(BF16).astype(F32)
    hidden_grad = down * row_scale
    gate_act_grad = hidden_grad * up * sigmoid * (1.0 + gate * (1.0 - sigmoid))
    prob_grad = live[:, :1] * jnp.sum(hidden * down, axis=1, keepdims=True)
    prob_row = jnp.sum(diagonal[...] * prob_grad, axis=0, keepdims=True)
    high = prob_row.astype(BF16).astype(F32)
    tail = jnp.concatenate([high, prob_row - high, jnp.zeros((6, prob_row.shape[1]), F32)], axis=0)
    tail = jnp.concatenate([tail, jnp.zeros((8, width - prob_row.shape[1]), F32)], axis=1)
    out[...] = jnp.concatenate([hidden * row_scale, gate_act_grad, hidden_grad * silu, tail], axis=0).astype(BF16)


def parts(a, b):
    a, b = a[...].astype(F32), b[...].astype(F32)
    rows = (a.shape[0] - 8) // 3
    both = [jnp.concatenate([a[q * rows : (q + 1) * rows], b[q * rows : (q + 1) * rows]], axis=0) for q in range(3)]
    return [x.astype(BF16) for x in both]


def slot_part(a, b, w_gate, w_up, column):
    _, gate_act_grad, up_act_grad = parts(a, b)
    at = pl.ds(column, a.shape[1])
    return dot(gate_act_grad, w_gate[:, at], (1, 1)) + dot(up_act_grad, w_up[:, at], (1, 1))


def weight_grad_copies(pieces, tok_t, grad_t, outs, held, sems):
    copies = []
    for a, b, column in pieces:
        down, gate, up = parts(a, b)
        for x, y, out in ((tok_t, gate, outs[0]), (tok_t, up, outs[1]), (grad_t, down, outs[2])):
            n = len(copies)
            held[n] = dot(x[...], y, (1, 0))
            copies.append(pltpu.make_async_copy(held.at[n], out.at[0, :, pl.ds(column, a.shape[1])], sems.at[n]))
            copies[n].start()
    return copies


def near_kernel(near0, near1, near2, near3, w_gate, w_up, tok_t, grad_t, out, gate_grad, up_grad, down_grad, held, sems):
    width = near0.shape[1]
    pieces = [(near0, near2, place(0, 0, width))]
    copies = weight_grad_copies(pieces, tok_t, grad_t, (gate_grad, up_grad, down_grad), held, sems)
    out[...] = slot_part(near0, near2, w_gate, w_up, place(0, 0, width)) + slot_part(
        near1, near3, w_gate, w_up, place(0, 1, width)
    )
    for copy in copies:
        copy.wait()


def slot_kernel(before, far, w_gate, w_up, out):
    width = far.shape[2]
    experts, slots, _ = out.shape
    total = before[...]
    for jy in range(2):
        total += slot_part(far.at[jy], far.at[2 + jy], w_gate, w_up, place(1, jy, width))
    for part in range(2):
        for j in range(experts // 2):
            start = (part * (experts // 2) + j) * slots
            out[(row_part() ^ part) * (experts // 2) + j] = total[start : start + slots].astype(BF16)


def weight_grad_kernel(near0, near1, near2, near3, far, tok_t, grad_t, *refs):
    gate_grad, up_grad, down_grad, prob_out, held, sems = refs[3:]
    width = far.shape[2]
    pieces = [(near1, near3, place(0, 1, width))]
    pieces += [(far.at[jy], far.at[2 + jy], place(1, jy, width)) for jy in range(2)]
    copies = weight_grad_copies(pieces, tok_t, grad_t, (gate_grad, up_grad, down_grad), held, sems)
    tail = jnp.zeros((8, width), F32)
    for chunk in (near0, near1, near2, near3, far.at[0], far.at[1], far.at[2], far.at[3]):
        tail += chunk[...].astype(F32)[-8:]
    prob = jnp.broadcast_to(tail[0:1] + tail[1:2], (8, width))
    share = prob_out.shape[1]
    shift = lax.rem(width - lax.axis_index("fsdp") * share, width)
    prob_out[...] = pltpu.roll(prob, shift, 1)[:1, :share]
    for copy in copies:
        copy.wait()


def token_grad_kernel(own, recv, onehot, out, held, sems):
    blocks = [own[...]] + [recv[j] for j in range(recv.shape[0])]
    slot_grad = jnp.concatenate([block.astype(F32) for block in blocks], axis=0).T.astype(BF16)
    count, _, width = held.shape
    copies = []
    for i in range(count):
        held[i] = dot(slot_grad, onehot[:, i * width : (i + 1) * width], (1, 0)).astype(BF16)
        copies.append(pltpu.make_async_copy(held.at[i], out.at[:, pl.ds(i * width, width)], sems.at[i]))
        copies[i].start()
    for copy in copies:
        copy.wait()


def local(tokens, out_grad, slot_rows, expert_counts, route_prob, w_gate, w_up, w_down):
    fsdp, experts = lax.axis_size("fsdp"), lax.axis_size("expert")
    steps = fsdp.bit_length() - 1
    token_count, features = tokens.shape
    _, _, slots = slot_rows.shape
    rows = experts * slots
    hidden = w_gate.shape[2]
    half, quarter = hidden // 2, hidden // 4
    def swap(x, *bits):
        mask = sum(1 << b for b in bits)
        return lax.ppermute(x, "fsdp", [(i, i ^ mask) for i in range(fsdp)])

    def to_expert(x):
        if experts == 2:
            return x[0], lax.ppermute(x[1], "expert", [(0, 1), (1, 0)])[None]
        moved = lax.all_to_all(x, "expert", split_axis=0, concat_axis=0, tiled=True)
        return moved[0], moved[1:]

    rows_out, onehot = pl.pallas_call(
        gather_kernel,
        out_shape=(
            jax.ShapeDtypeStruct((experts, 2, slots, features), BF16),
            jax.ShapeDtypeStruct((rows, token_count), BF16),
        ),
        in_specs=[HBM] * 3,
        out_specs=(VMEM, VMEM),
        scratch_shapes=[
            pltpu.SMEM((experts, slots), jnp.int32),
            pltpu.VMEM((features, token_count), BF16),
            pltpu.VMEM((features, token_count), BF16),
            pltpu.VMEM((rows, token_count), F32),
            pltpu.SemaphoreType.DMA((3,)),
        ],
        compiler_params=PARAMS,
        name="gather_rows",
    )(*(in_hbm(x) for x in (slot_rows[0], tokens.T, out_grad.T)))
    own, recv = to_expert(rows_out)
    weights = pl.pallas_call(
        load_kernel,
        out_shape=(jax.ShapeDtypeStruct((features, hidden), BF16),) * 3,
        in_specs=[VMEM] + [HBM] * 3,
        out_specs=(VMEM,) * 3,
        scratch_shapes=[pltpu.SemaphoreType.DMA((3,))],
        compiler_params=PARAMS,
        cost_estimate=pl.CostEstimate(flops=0, bytes_accessed=6 * features * hidden, transcendentals=0),
        name="load_weights",
    )(own, *(in_hbm(w) for w in (w_gate, w_up, w_down)))

    def partial(side):
        return pl.pallas_call(
            functools.partial(partial_kernel, side),
            out_shape=jax.ShapeDtypeStruct((4, 3 * rows // 2, quarter), F32),
            in_specs=[VMEM] * 5,
            out_specs=VMEM,
            compiler_params=PARAMS,
            cost_estimate=pl.CostEstimate(
                flops=6 * rows * features * half, bytes_accessed=3 * features * half * 2, transcendentals=0
            ),
            name="partial_sums",
        )(own, recv, *weights)

    arrived = swap(partial(1), 0)
    kept = partial(0)
    turned_shape = jax.ShapeDtypeStruct((features, rows), BF16)
    fact_shape = jax.ShapeDtypeStruct((rows // 2, 128), F32)
    diagonal_shape = jax.ShapeDtypeStruct((rows // 2, (rows + 127) // 128 * 128), F32)
    tok_t, grad_t, scale, live, diagonal = pl.pallas_call(
        rows_kernel,
        out_shape=(turned_shape, turned_shape, fact_shape, fact_shape, diagonal_shape),
        in_specs=[SMEM] + [VMEM] * 3,
        out_specs=(VMEM,) * 5,
        compiler_params=PARAMS,
        cost_estimate=pl.CostEstimate(flops=0, bytes_accessed=8 * features * rows, transcendentals=0),
        name="row_facts",
    )(expert_counts[0], own, recv, route_prob)
    coded_shape = jax.ShapeDtypeStruct((3 * rows // 2 + 8, quarter), F32)
    total, power, *sent = pl.pallas_call(
        add_kernel,
        out_shape=(
            jax.ShapeDtypeStruct((3 * rows // 2, quarter), F32),
            jax.ShapeDtypeStruct((8, quarter), F32),
        )
        + (coded_shape,) * 3,
        in_specs=[VMEM] * 2,
        out_specs=(VMEM,) * 5,
        compiler_params=PARAMS,
        name="add",
    )(kept, arrived)
    arrived = [swap(x.astype(F16), *bits) for x, bits in zip(sent, ((1,), (2,), (1, 2)))]
    for x in arrived:
        chunk, its_power = decoded(x)
        total, power = total + chunk, jnp.maximum(power, its_power)
    power += 2.0
    for b in range(3, steps):
        arrived, its_power = decoded(swap(coded(total, power).astype(F16), b))
        if b < steps - 1:
            total, power = total + arrived, jnp.maximum(power, its_power) + 1.0
    acts = pl.pallas_call(
        hidden_kernel,
        out_shape=jax.ShapeDtypeStruct((3 * rows // 2 + 8, quarter), BF16),
        in_specs=[VMEM] * 5,
        out_specs=VMEM,
        compiler_params=PARAMS,
        name="hidden",
    )(scale, live, diagonal, total, arrived)
    near = [acts, swap(acts, 1), swap(acts, 2), swap(acts, 1, 2)]
    far = swap(jnp.stack(near), 0)

    grad_shape = jax.ShapeDtypeStruct((1, features, hidden), F32)

    def held(count):
        return [pltpu.VMEM((count, features, quarter), F32), pltpu.SemaphoreType.DMA((count,))]

    near_slot, *grads = pl.pallas_call(
        near_kernel,
        out_shape=(jax.ShapeDtypeStruct((rows, features), F32),) + (grad_shape,) * 3,
        in_specs=[VMEM] * 8,
        out_specs=(VMEM,) + (HBM,) * 3,
        scratch_shapes=held(3),
        compiler_params=PARAMS,
        cost_estimate=pl.CostEstimate(
            flops=4 * rows * features * hidden, bytes_accessed=3 * features * hidden, transcendentals=0
        ),
        name="near_piece",
    )(*near, weights[0], weights[1], tok_t, grad_t)
    slot_grad = pl.pallas_call(
        slot_kernel,
        out_shape=jax.ShapeDtypeStruct((experts, slots, features), BF16),
        in_specs=[VMEM] * 4,
        out_specs=VMEM,
        compiler_params=PARAMS,
        name="slot_grad",
    )(near_slot, far, weights[0], weights[1])
    slot_own, slot_recv = to_expert(slot_grad)
    gate_grad, up_grad, down_grad, prob_grad = pl.pallas_call(
        weight_grad_kernel,
        out_shape=(grad_shape,) * 3 + (jax.ShapeDtypeStruct((1, rows // fsdp), F32),),
        in_specs=[VMEM] * 7 + [HBM] * 3,
        out_specs=(HBM,) * 3 + (VMEM,),
        scratch_shapes=held(9),
        input_output_aliases={7 + i: i for i in range(3)},
        compiler_params=PARAMS,
        cost_estimate=pl.CostEstimate(
            flops=4 * rows * features * hidden, bytes_accessed=9 * features * hidden, transcendentals=0
        ),
        name="weight_grads",
    )(*near, far, tok_t, grad_t, *grads)

    token_grad = pl.pallas_call(
        token_grad_kernel,
        out_shape=jax.ShapeDtypeStruct((features, token_count), BF16),
        in_specs=[VMEM] * 3,
        out_specs=HBM,
        scratch_shapes=[pltpu.VMEM((4, features, token_count // 4), BF16), pltpu.SemaphoreType.DMA((4,))],
        compiler_params=PARAMS,
        name="token_grad",
    )(slot_own, slot_recv, onehot).T
    return (token_grad, gate_grad, up_grad, down_grad, prob_grad)


def solution(mesh):
    return jax.shard_map(
        local,
        mesh=mesh,
        in_specs=(
            P("expert", "fsdp"),
            P("expert", "fsdp"),
            P("expert", None, None),
            P("expert", None),
            P("expert", None),
            P("expert", "fsdp", None),
            P("expert", "fsdp", None),
            P("expert", "fsdp", None),
        ),
        out_specs=(
            P("expert", "fsdp"),
            P("expert", "fsdp", None),
            P("expert", "fsdp", None),
            P("expert", "fsdp", None),
            P("expert", "fsdp"),
        ),
        check_vma=False,
    )
```

```python
import functools

import jax
import jax.numpy as jnp
from jax import lax
from jax.experimental import pallas as pl
from jax.experimental.pallas import tpu as pltpu
from jax.sharding import PartitionSpec as P

BF16 = jnp.bfloat16
F32 = jnp.float32
F16 = jnp.float16
VMEM = pl.BlockSpec(memory_space=pltpu.VMEM)
HBM = pl.BlockSpec(memory_space=pltpu.HBM)
SMEM = pl.BlockSpec(memory_space=pltpu.SMEM)
PARAMS = pltpu.CompilerParams(vmem_limit_bytes=40 * 2**20)

def in_hbm(x):
    return pltpu.with_memory_space_constraint(x, pltpu.HBM)


def dot(a, b, contract):
    return lax.dot_general(a, b, ((contract[0:1], contract[1:2]), ((), ())), preferred_element_type=F32)


def place(side, jy, width):
    me = lax.axis_index("fsdp")
    half = (me & 1) ^ side
    return pl.multiple_of((half * 2 + (((me >> 1) & 1) ^ jy)) * width, 128)


def place_in_half(jy, width):
    return pl.multiple_of((((lax.axis_index("fsdp") >> 1) & 1) ^ jy) * width, 128)


def half_copies(side, weights, to, sems):
    width = to.shape[2]
    at = pl.ds(pl.multiple_of(((lax.axis_index("fsdp") & 1) ^ side) * width, 128), width)
    return [pltpu.make_async_copy(w.at[0, :, at], to.at[i], sems.at[i]) for i, w in enumerate(weights)]


def row_part():
    return (lax.axis_index("fsdp") >> 2) & 1


def first_expert(experts):
    return lax.axis_index("expert") if experts == 2 else 0


def gather_kernel(slot_rows_hbm, tokens_hbm, grads_hbm, *refs):
    weights, (rows_out, onehot_out, far_out, slot_rows, tokens_t, grads_t, onehot_f, sems, far_sems) = refs[:3], refs[3:]
    copies = [
        pltpu.make_async_copy(source, to, sems.at[i])
        for i, (source, to) in enumerate(((slot_rows_hbm, slot_rows), (tokens_hbm, tokens_t), (grads_hbm, grads_t)))
    ]
    far_copies = half_copies(1, weights, far_out, far_sems)
    for copy in copies + far_copies:
        copy.start()
    experts, slots = slot_rows.shape
    count = tokens_t.shape[1]
    first = first_expert(experts)
    lane = lax.broadcasted_iota(jnp.int32, (8, count), 1)
    sub = lax.broadcasted_iota(jnp.int32, (8, count), 0)
    copies[0].wait()
    for j in range(experts):
        expert = lax.rem(first + j, experts)
        for base in range(0, slots, 8):
            picked = jnp.zeros((8, count), jnp.int32)
            for r in range(8):
                picked = jnp.where(sub == r, slot_rows[expert, base + r], picked)
            onehot_f[pl.ds(j * slots + base, 8), :] = (picked == lane).astype(F32)
    onehot = onehot_f[...].astype(BF16)
    onehot_out[...] = onehot
    for kind, source in enumerate((tokens_t, grads_t)):
        copies[1 + kind].wait()
        rows = dot(onehot, source[...], (1, 1))
        for j in range(experts):
            rows_out[j, kind] = rows[j * slots : (j + 1) * slots].astype(BF16)
    for copy in far_copies:
        copy.wait()


def load_kernel(after, w_gate, w_up, w_down, out, sems):
    del after
    copies = half_copies(0, (w_gate, w_up, w_down), out, sems)
    for copy in copies:
        copy.start()
    for copy in copies:
        copy.wait()


def stacked_rows(own, recv, kind):
    blocks = [own[kind]] + [recv[j, kind] for j in range(recv.shape[0])]
    return jnp.concatenate([block.astype(F32) for block in blocks], axis=0)


def partial_sums(own, recv, weights, width, jy, q):
    rows = stacked_rows(own, recv, q // 2).astype(BF16)
    return dot(rows, weights[q, :, pl.ds(place_in_half(jy, width), width)], (1, 0))


def partial_kernel(own, recv, weights, out):
    chunk_rows, width = out.shape[1] // 3, out.shape[2]
    for jy in range(2):
        for q in range(3):
            sums = partial_sums(own, recv, weights, width, jy, q)
            for part in range(2):
                chunk = (row_part() ^ part) * 2 + jy
                out[chunk, pl.ds(q * chunk_rows, chunk_rows), :] = sums[part * chunk_rows : (part + 1) * chunk_rows]


def rows_kernel(counts, own, recv, prob, tok_t, grad_t, scale_out, live_out, diagonal_out):
    part0 = row_part()
    rows, lanes = diagonal_out.shape
    for to, x in ((tok_t, stacked_rows(own, recv, 0)), (grad_t, stacked_rows(own, recv, 1))):
        low, high = x[:rows], x[rows:]
        near, far = jnp.where(part0 == 0, low, high), jnp.where(part0 == 0, high, low)
        to[...] = jnp.concatenate([near, far], axis=0).T.astype(BF16)
    experts = counts.shape[0]
    slots = 2 * rows // experts
    first = first_expert(experts)
    row = lax.broadcasted_iota(jnp.int32, (rows, lanes), 0) + part0 * rows
    lane = lax.broadcasted_iota(jnp.int32, (rows, lanes), 1)
    slot, home, live_count = row, row, row
    for j in range(experts):
        source = lax.rem(first + j, experts)
        inside = (row >= j * slots) & (row < (j + 1) * slots)
        slot = jnp.where(inside, row - j * slots, slot)
        home = jnp.where(inside, source * slots + row - j * slots, home)
        live_count = jnp.where(inside, counts[source], live_count)
    live = (slot < live_count).astype(F32)
    diagonal = lane == home
    probs = jnp.concatenate([prob[...], jnp.zeros((1, lanes - 2 * rows), F32)], axis=1)
    row_prob = jnp.sum(jnp.where(diagonal, probs, 0.0), axis=1, keepdims=True)
    scale_out[...] = row_prob * live[:, :128]
    live_out[...] = live[:, :128]
    diagonal_out[...] = diagonal.astype(F32)


def add_kernel(kept, own, recv, weights, first, power_out, *refs):
    outs, summed = refs[:-1], refs[-1]
    partial_kernel(own, recv, weights, summed)
    rows = first.shape[0] // 3
    width = first.shape[1]
    chunks = [kept[j] + summed[j] for j in range(4)]
    first[...] = chunks[0]
    powers = []
    for q in range(3):
        most = functools.reduce(jnp.maximum, [jnp.abs(x[q * rows : (q + 1) * rows]) for x in chunks])
        most = jnp.max(jnp.max(most, axis=0, keepdims=True), axis=1, keepdims=True)
        most = jnp.maximum(jnp.broadcast_to(most, (1, width)), 1e-30)
        powers.append(jnp.ceil(jnp.log2(most)) - 14.0)
    power_out[...] = jnp.concatenate(powers + [jnp.zeros((5, width), F32)], axis=0)
    for x, out in zip(chunks[1:], outs):
        for q in range(3):
            out[pl.ds(q * rows, rows), :] = x[q * rows : (q + 1) * rows] * jnp.exp2(-powers[q])
        out[pl.ds(3 * rows, 8), :] = power_out[...]


def scaled(x, power):
    rows = x.shape[0] // 3
    return (x.reshape(3, rows, -1) * jnp.exp2(power[:3])[:, None]).reshape(x.shape)


def coded(x, power):
    return jnp.concatenate([scaled(x, -power), power], axis=0)


def decoded(x):
    x = x.astype(F32)
    return scaled(x[:-8], x[-8:]), x[-8:]


def hidden_kernel(scale, live, diagonal, sums, recv, out):
    rows = sums.shape[0] // 3
    width = sums.shape[1]
    total = sums[...] + recv[...]
    gate, up, down = total[:rows], total[rows : 2 * rows], total[2 * rows :]
    row_scale = jnp.concatenate([scale[...]] * (width // 128), axis=1)
    sigmoid = jax.nn.sigmoid(gate)
    silu = gate * sigmoid
    hidden = (silu * up).astype(BF16).astype(F32)
    hidden_grad = down * row_scale
    gate_act_grad = hidden_grad * up * sigmoid * (1.0 + gate * (1.0 - sigmoid))
    prob_grad = live[:, :1] * jnp.sum(hidden * down, axis=1, keepdims=True)
    prob_row = jnp.sum(diagonal[...] * prob_grad, axis=0, keepdims=True)
    high = prob_row.astype(BF16).astype(F32)
    tail = jnp.concatenate([high, prob_row - high, jnp.zeros((6, prob_row.shape[1]), F32)], axis=0)
    tail = jnp.concatenate([tail, jnp.zeros((8, width - prob_row.shape[1]), F32)], axis=1)
    out[...] = jnp.concatenate([hidden * row_scale, gate_act_grad, hidden_grad * silu, tail], axis=0).astype(BF16)


def parts(a, b):
    a, b = a[...].astype(F32), b[...].astype(F32)
    rows = (a.shape[0] - 8) // 3
    both = [jnp.concatenate([a[q * rows : (q + 1) * rows], b[q * rows : (q + 1) * rows]], axis=0) for q in range(3)]
    return [x.astype(BF16) for x in both]


def slot_part(a, b, weights, jy):
    _, gate_act_grad, up_act_grad = parts(a, b)
    at = pl.ds(place_in_half(jy, a.shape[1]), a.shape[1])
    return dot(gate_act_grad, weights[0, :, at], (1, 1)) + dot(up_act_grad, weights[1, :, at], (1, 1))


def weight_grad_copies(pieces, tok_t, grad_t, outs, held, sems):
    copies = []
    for a, b, column in pieces:
        down, gate, up = parts(a, b)
        for x, y, out in ((tok_t, gate, outs[0]), (tok_t, up, outs[1]), (grad_t, down, outs[2])):
            n = len(copies)
            held[n] = dot(x[...], y, (1, 0))
            copies.append(pltpu.make_async_copy(held.at[n], out.at[0, :, pl.ds(column, a.shape[1])], sems.at[n]))
            copies[n].start()
    return copies


def near_kernel(near0, near1, near2, near3, weights, tok_t, grad_t, out, gate_grad, up_grad, down_grad, held, sems):
    width = near0.shape[1]
    pieces = [(near0, near2, place(0, 0, width))]
    copies = weight_grad_copies(pieces, tok_t, grad_t, (gate_grad, up_grad, down_grad), held, sems)
    out[...] = slot_part(near0, near2, weights, 0) + slot_part(near1, near3, weights, 1)
    for copy in copies:
        copy.wait()


def slot_kernel(before, far, weights, out):
    experts, slots, _ = out.shape
    total = before[...]
    for jy in range(2):
        total += slot_part(far.at[jy], far.at[2 + jy], weights, jy)
    for part in range(2):
        for j in range(experts // 2):
            start = (part * (experts // 2) + j) * slots
            out[(row_part() ^ part) * (experts // 2) + j] = total[start : start + slots].astype(BF16)


def weight_grad_kernel(near0, near1, near2, near3, far, tok_t, grad_t, *refs):
    gate_grad, up_grad, down_grad, prob_out, held, sems = refs[3:]
    width = far.shape[2]
    pieces = [(near1, near3, place(0, 1, width))]
    pieces += [(far.at[jy], far.at[2 + jy], place(1, jy, width)) for jy in range(2)]
    copies = weight_grad_copies(pieces, tok_t, grad_t, (gate_grad, up_grad, down_grad), held, sems)
    tail = jnp.zeros((8, width), F32)
    for chunk in (near0, near1, near2, near3, far.at[0], far.at[1], far.at[2], far.at[3]):
        tail += chunk[...].astype(F32)[-8:]
    prob = jnp.broadcast_to(tail[0:1] + tail[1:2], (8, width))
    share = prob_out.shape[1]
    shift = lax.rem(width - lax.axis_index("fsdp") * share, width)
    prob_out[...] = pltpu.roll(prob, shift, 1)[:1, :share]
    for copy in copies:
        copy.wait()


def token_grad_kernel(own, recv, onehot, out, held, sems):
    blocks = [own[...]] + [recv[j] for j in range(recv.shape[0])]
    slot_grad = jnp.concatenate([block.astype(F32) for block in blocks], axis=0).T.astype(BF16)
    count, _, width = held.shape
    copies = []
    for i in range(count):
        held[i] = dot(slot_grad, onehot[:, i * width : (i + 1) * width], (1, 0)).astype(BF16)
        copies.append(pltpu.make_async_copy(held.at[i], out.at[:, pl.ds(i * width, width)], sems.at[i]))
        copies[i].start()
    for copy in copies:
        copy.wait()


def local(tokens, out_grad, slot_rows, expert_counts, route_prob, w_gate, w_up, w_down):
    fsdp, experts = lax.axis_size("fsdp"), lax.axis_size("expert")
    steps = fsdp.bit_length() - 1
    token_count, features = tokens.shape
    _, _, slots = slot_rows.shape
    rows = experts * slots
    hidden = w_gate.shape[2]
    half, quarter = hidden // 2, hidden // 4
    def swap(x, *bits):
        mask = sum(1 << b for b in bits)
        return lax.ppermute(x, "fsdp", [(i, i ^ mask) for i in range(fsdp)])

    def to_expert(x):
        if experts == 2:
            return x[0], lax.ppermute(x[1], "expert", [(0, 1), (1, 0)])[None]
        moved = lax.all_to_all(x, "expert", split_axis=0, concat_axis=0, tiled=True)
        return moved[0], moved[1:]

    half_shape = jax.ShapeDtypeStruct((3, features, half), BF16)
    rows_out, onehot, far_weights = pl.pallas_call(
        gather_kernel,
        out_shape=(
            jax.ShapeDtypeStruct((experts, 2, slots, features), BF16),
            jax.ShapeDtypeStruct((rows, token_count), BF16),
            half_shape,
        ),
        in_specs=[HBM] * 6,
        out_specs=(VMEM,) * 3,
        scratch_shapes=[
            pltpu.SMEM((experts, slots), jnp.int32),
            pltpu.VMEM((features, token_count), BF16),
            pltpu.VMEM((features, token_count), BF16),
            pltpu.VMEM((rows, token_count), F32),
            pltpu.SemaphoreType.DMA((3,)),
            pltpu.SemaphoreType.DMA((3,)),
        ],
        compiler_params=PARAMS,
        name="gather_rows",
    )(*(in_hbm(x) for x in (slot_rows[0], tokens.T, out_grad.T, w_gate, w_up, w_down)))
    own, recv = to_expert(rows_out)
    if experts == 2:
        crossed = [(f * 2 + x, (f ^ 1) * 2 + 1 - x) for f in range(fsdp) for x in range(2)]
        other_recv = lax.ppermute(rows_out[1], ("fsdp", "expert"), crossed)[None]
    else:
        other_recv = swap(recv, 0)
    other_own = swap(own, 0)
    other_weights = swap(far_weights, 0)
    near_weights = pl.pallas_call(
        load_kernel,
        out_shape=half_shape,
        in_specs=[VMEM] + [HBM] * 3,
        out_specs=VMEM,
        scratch_shapes=[pltpu.SemaphoreType.DMA((3,))],
        compiler_params=PARAMS,
        cost_estimate=pl.CostEstimate(flops=0, bytes_accessed=6 * features * half, transcendentals=0),
        name="load_weights",
    )(own, *(in_hbm(w) for w in (w_gate, w_up, w_down)))
    kept = pl.pallas_call(
        partial_kernel,
        out_shape=jax.ShapeDtypeStruct((4, 3 * rows // 2, quarter), F32),
        in_specs=[VMEM] * 3,
        out_specs=VMEM,
        compiler_params=PARAMS,
        cost_estimate=pl.CostEstimate(
            flops=6 * rows * features * half, bytes_accessed=6 * features * half, transcendentals=0
        ),
        name="partial_sums",
    )(own, recv, near_weights)
    turned_shape = jax.ShapeDtypeStruct((features, rows), BF16)
    fact_shape = jax.ShapeDtypeStruct((rows // 2, 128), F32)
    diagonal_shape = jax.ShapeDtypeStruct((rows // 2, (rows + 127) // 128 * 128), F32)
    tok_t, grad_t, scale, live, diagonal = pl.pallas_call(
        rows_kernel,
        out_shape=(turned_shape, turned_shape, fact_shape, fact_shape, diagonal_shape),
        in_specs=[SMEM] + [VMEM] * 3,
        out_specs=(VMEM,) * 5,
        compiler_params=PARAMS,
        cost_estimate=pl.CostEstimate(flops=0, bytes_accessed=8 * features * rows, transcendentals=0),
        name="row_facts",
    )(expert_counts[0], own, recv, route_prob)
    coded_shape = jax.ShapeDtypeStruct((3 * rows // 2 + 8, quarter), F32)
    total, power, *sent = pl.pallas_call(
        add_kernel,
        out_shape=(
            jax.ShapeDtypeStruct((3 * rows // 2, quarter), F32),
            jax.ShapeDtypeStruct((8, quarter), F32),
        )
        + (coded_shape,) * 3,
        in_specs=[VMEM] * 4,
        out_specs=(VMEM,) * 5,
        scratch_shapes=[pltpu.VMEM(kept.shape, F32)],
        compiler_params=PARAMS,
        name="add_other_core",
    )(kept, other_own, other_recv, other_weights)
    arrived = [swap(x.astype(F16), *bits) for x, bits in zip(sent, ((1,), (2,), (1, 2)))]
    for x in arrived:
        chunk, its_power = decoded(x)
        total, power = total + chunk, jnp.maximum(power, its_power)
    power += 2.0
    for b in range(3, steps):
        arrived, its_power = decoded(swap(coded(total, power).astype(F16), b))
        if b < steps - 1:
            total, power = total + arrived, jnp.maximum(power, its_power) + 1.0
    acts = pl.pallas_call(
        hidden_kernel,
        out_shape=jax.ShapeDtypeStruct((3 * rows // 2 + 8, quarter), BF16),
        in_specs=[VMEM] * 5,
        out_specs=VMEM,
        compiler_params=PARAMS,
        name="hidden",
    )(scale, live, diagonal, total, arrived)
    near = [acts, swap(acts, 1), swap(acts, 2), swap(acts, 1, 2)]
    far = swap(jnp.stack(near), 0)

    grad_shape = jax.ShapeDtypeStruct((1, features, hidden), F32)

    def held(count):
        return [pltpu.VMEM((count, features, quarter), F32), pltpu.SemaphoreType.DMA((count,))]

    near_slot, *grads = pl.pallas_call(
        near_kernel,
        out_shape=(jax.ShapeDtypeStruct((rows, features), F32),) + (grad_shape,) * 3,
        in_specs=[VMEM] * 7,
        out_specs=(VMEM,) + (HBM,) * 3,
        scratch_shapes=held(3),
        compiler_params=PARAMS,
        cost_estimate=pl.CostEstimate(
            flops=4 * rows * features * hidden, bytes_accessed=3 * features * hidden, transcendentals=0
        ),
        name="near_piece",
    )(*near, near_weights, tok_t, grad_t)
    slot_grad = pl.pallas_call(
        slot_kernel,
        out_shape=jax.ShapeDtypeStruct((experts, slots, features), BF16),
        in_specs=[VMEM] * 3,
        out_specs=VMEM,
        compiler_params=PARAMS,
        name="slot_grad",
    )(near_slot, far, far_weights)
    slot_own, slot_recv = to_expert(slot_grad)
    gate_grad, up_grad, down_grad, prob_grad = pl.pallas_call(
        weight_grad_kernel,
        out_shape=(grad_shape,) * 3 + (jax.ShapeDtypeStruct((1, rows // fsdp), F32),),
        in_specs=[VMEM] * 7 + [HBM] * 3,
        out_specs=(HBM,) * 3 + (VMEM,),
        scratch_shapes=held(9),
        input_output_aliases={7 + i: i for i in range(3)},
        compiler_params=PARAMS,
        cost_estimate=pl.CostEstimate(
            flops=4 * rows * features * hidden, bytes_accessed=9 * features * hidden, transcendentals=0
        ),
        name="weight_grads",
    )(*near, far, tok_t, grad_t, *grads)

    token_grad = pl.pallas_call(
        token_grad_kernel,
        out_shape=jax.ShapeDtypeStruct((features, token_count), BF16),
        in_specs=[VMEM] * 3,
        out_specs=HBM,
        scratch_shapes=[pltpu.VMEM((4, features, token_count // 4), BF16), pltpu.SemaphoreType.DMA((4,))],
        compiler_params=PARAMS,
        name="token_grad",
    )(slot_own, slot_recv, onehot).T
    return (token_grad, gate_grad, up_grad, down_grad, prob_grad)


def solution(mesh):
    return jax.shard_map(
        local,
        mesh=mesh,
        in_specs=(
            P("expert", "fsdp"),
            P("expert", "fsdp"),
            P("expert", None, None),
            P("expert", None),
            P("expert", None),
            P("expert", "fsdp", None),
            P("expert", "fsdp", None),
            P("expert", "fsdp", None),
        ),
        out_specs=(
            P("expert", "fsdp"),
            P("expert", "fsdp", None),
            P("expert", "fsdp", None),
            P("expert", "fsdp", None),
            P("expert", "fsdp"),
        ),
        check_vma=False,
    )
```

```python
import functools

import jax
import jax.numpy as jnp
from jax import lax
from jax.experimental import pallas as pl
from jax.experimental.pallas import tpu as pltpu
from jax.sharding import PartitionSpec as P

BF16 = jnp.bfloat16
F32 = jnp.float32
F16 = jnp.float16
VMEM = pl.BlockSpec(memory_space=pltpu.VMEM)
HBM = pl.BlockSpec(memory_space=pltpu.HBM)
SMEM = pl.BlockSpec(memory_space=pltpu.SMEM)
PARAMS = pltpu.CompilerParams(vmem_limit_bytes=40 * 2**20)

def in_hbm(x):
    return pltpu.with_memory_space_constraint(x, pltpu.HBM)


def dot(a, b, contract):
    return lax.dot_general(a, b, ((contract[0:1], contract[1:2]), ((), ())), preferred_element_type=F32)


def place(side, jy, width):
    me = lax.axis_index("fsdp")
    half = (me & 1) ^ side
    return pl.multiple_of((half * 2 + (((me >> 1) & 1) ^ jy)) * width, 128)


def place_in_half(jy, width):
    return pl.multiple_of((((lax.axis_index("fsdp") >> 1) & 1) ^ jy) * width, 128)


def half_copies(side, weights, to, sems):
    width = to.shape[2]
    at = pl.ds(pl.multiple_of(((lax.axis_index("fsdp") & 1) ^ side) * width, 128), width)
    return [pltpu.make_async_copy(w.at[0, :, at], to.at[i], sems.at[i]) for i, w in enumerate(weights)]


def row_part():
    return (lax.axis_index("fsdp") >> 2) & 1


def first_expert(experts):
    return lax.axis_index("expert") if experts == 2 else 0


def gather_kernel(slot_rows_hbm, tokens_hbm, grads_hbm, *refs):
    weights, (rows_out, onehot_out, far_out, slot_rows, tokens_t, grads_t, onehot_f, sems, far_sems) = refs[:3], refs[3:]
    copies = [
        pltpu.make_async_copy(source, to, sems.at[i])
        for i, (source, to) in enumerate(((slot_rows_hbm, slot_rows), (tokens_hbm, tokens_t), (grads_hbm, grads_t)))
    ]
    far_copies = half_copies(1, weights, far_out, far_sems)
    for copy in copies + far_copies:
        copy.start()
    experts, slots = slot_rows.shape
    count = tokens_t.shape[1]
    first = first_expert(experts)
    lane = lax.broadcasted_iota(jnp.int32, (8, count), 1)
    sub = lax.broadcasted_iota(jnp.int32, (8, count), 0)
    copies[0].wait()
    for j in range(experts):
        expert = lax.rem(first + j, experts)
        for base in range(0, slots, 8):
            picked = jnp.zeros((8, count), jnp.int32)
            for r in range(8):
                picked = jnp.where(sub == r, slot_rows[expert, base + r], picked)
            onehot_f[pl.ds(j * slots + base, 8), :] = (picked == lane).astype(F32)
    onehot = onehot_f[...].astype(BF16)
    onehot_out[...] = onehot
    for kind, source in enumerate((tokens_t, grads_t)):
        copies[1 + kind].wait()
        rows = dot(onehot, source[...], (1, 1))
        for j in range(experts):
            rows_out[j, kind] = rows[j * slots : (j + 1) * slots].astype(BF16)
    for copy in far_copies:
        copy.wait()


def load_kernel(after, w_gate, w_up, w_down, out, sems):
    del after
    copies = half_copies(0, (w_gate, w_up, w_down), out, sems)
    for copy in copies:
        copy.start()
    for copy in copies:
        copy.wait()


def stacked_rows(own, recv, kind):
    blocks = [own[kind]] + [recv[j, kind] for j in range(recv.shape[0])]
    return jnp.concatenate([block.astype(F32) for block in blocks], axis=0)


def partial_sums(own, recv, weights, width, jy, q):
    rows = stacked_rows(own, recv, q // 2).astype(BF16)
    return dot(rows, weights[q, :, pl.ds(place_in_half(jy, width), width)], (1, 0))


def partial_kernel(own, recv, weights, out):
    chunk_rows, width = out.shape[1] // 3, out.shape[2]
    for jy in range(2):
        for q in range(3):
            sums = partial_sums(own, recv, weights, width, jy, q)
            for part in range(2):
                chunk = (row_part() ^ part) * 2 + jy
                out[chunk, pl.ds(q * chunk_rows, chunk_rows), :] = sums[part * chunk_rows : (part + 1) * chunk_rows]


def rows_kernel(counts, own, recv, prob, tok_t, grad_t, scale_out, live_out, diagonal_out):
    part0 = row_part()
    rows, lanes = diagonal_out.shape
    for to, x in ((tok_t, stacked_rows(own, recv, 0)), (grad_t, stacked_rows(own, recv, 1))):
        low, high = x[:rows], x[rows:]
        near, far = jnp.where(part0 == 0, low, high), jnp.where(part0 == 0, high, low)
        to[...] = jnp.concatenate([near, far], axis=0).T.astype(BF16)
    experts = counts.shape[0]
    slots = 2 * rows // experts
    first = first_expert(experts)
    row = lax.broadcasted_iota(jnp.int32, (rows, lanes), 0) + part0 * rows
    lane = lax.broadcasted_iota(jnp.int32, (rows, lanes), 1)
    slot, home, live_count = row, row, row
    for j in range(experts):
        source = lax.rem(first + j, experts)
        inside = (row >= j * slots) & (row < (j + 1) * slots)
        slot = jnp.where(inside, row - j * slots, slot)
        home = jnp.where(inside, source * slots + row - j * slots, home)
        live_count = jnp.where(inside, counts[source], live_count)
    live = (slot < live_count).astype(F32)
    diagonal = lane == home
    probs = jnp.concatenate([prob[...], jnp.zeros((1, lanes - 2 * rows), F32)], axis=1)
    row_prob = jnp.sum(jnp.where(diagonal, probs, 0.0), axis=1, keepdims=True)
    scale_out[...] = row_prob * live[:, :128]
    live_out[...] = live[:, :128]
    diagonal_out[...] = diagonal.astype(F32)


def add_kernel(kept, own, recv, weights, first, power_out, *refs):
    outs, summed = refs[:-1], refs[-1]
    partial_kernel(own, recv, weights, summed)
    rows = first.shape[0] // 3
    width = first.shape[1]
    chunks = [kept[j] + summed[j] for j in range(4)]
    first[...] = chunks[0]
    powers = []
    for q in range(3):
        most = functools.reduce(jnp.maximum, [jnp.abs(x[q * rows : (q + 1) * rows]) for x in chunks])
        most = jnp.max(jnp.max(most, axis=0, keepdims=True), axis=1, keepdims=True)
        most = jnp.maximum(jnp.broadcast_to(most, (1, width)), 1e-30)
        powers.append(jnp.ceil(jnp.log2(most)) - 14.0)
    power_out[...] = jnp.concatenate(powers + [jnp.zeros((5, width), F32)], axis=0)
    for x, out in zip(chunks[1:], outs):
        for q in range(3):
            out[pl.ds(q * rows, rows), :] = x[q * rows : (q + 1) * rows] * jnp.exp2(-powers[q])
        out[pl.ds(3 * rows, 8), :] = power_out[...]


def scaled(x, power):
    rows = x.shape[0] // 3
    return (x.reshape(3, rows, -1) * jnp.exp2(power[:3])[:, None]).reshape(x.shape)


def coded(x, power):
    return jnp.concatenate([scaled(x, -power), power], axis=0)


def decoded(x):
    x = x.astype(F32)
    return scaled(x[:-8], x[-8:]), x[-8:]


def hidden_kernel(scale, live, diagonal, sums, recv, out):
    rows = sums.shape[0] // 3
    width = sums.shape[1]
    total = sums[...] + recv[...]
    gate, up, down = total[:rows], total[rows : 2 * rows], total[2 * rows :]
    row_scale = jnp.concatenate([scale[...]] * (width // 128), axis=1)
    sigmoid = jax.nn.sigmoid(gate)
    silu = gate * sigmoid
    hidden = (silu * up).astype(BF16).astype(F32)
    hidden_grad = down * row_scale
    gate_act_grad = hidden_grad * up * sigmoid * (1.0 + gate * (1.0 - sigmoid))
    prob_grad = live[:, :1] * jnp.sum(hidden * down, axis=1, keepdims=True)
    prob_row = jnp.sum(diagonal[...] * prob_grad, axis=0, keepdims=True)
    high = prob_row.astype(BF16).astype(F32)
    tail = jnp.concatenate([high, prob_row - high, jnp.zeros((6, prob_row.shape[1]), F32)], axis=0)
    tail = jnp.concatenate([tail, jnp.zeros((8, width - prob_row.shape[1]), F32)], axis=1)
    out[...] = jnp.concatenate([hidden * row_scale, gate_act_grad, hidden_grad * silu, tail], axis=0).astype(BF16)


def parts(a, b):
    a, b = a[...].astype(F32), b[...].astype(F32)
    rows = (a.shape[0] - 8) // 3
    both = [jnp.concatenate([a[q * rows : (q + 1) * rows], b[q * rows : (q + 1) * rows]], axis=0) for q in range(3)]
    return [x.astype(BF16) for x in both]


def slot_part(a, b, weights, jy):
    _, gate_act_grad, up_act_grad = parts(a, b)
    at = pl.ds(place_in_half(jy, a.shape[1]), a.shape[1])
    return dot(gate_act_grad, weights[0, :, at], (1, 1)) + dot(up_act_grad, weights[1, :, at], (1, 1))


def weight_grad_copies(pieces, tok_t, grad_t, outs, held, sems):
    copies = []
    for a, b, column in pieces:
        down, gate, up = parts(a, b)
        for x, y, out in ((tok_t, gate, outs[0]), (tok_t, up, outs[1]), (grad_t, down, outs[2])):
            n = len(copies)
            held[n] = dot(x[...], y, (1, 0))
            copies.append(pltpu.make_async_copy(held.at[n], out.at[0, :, pl.ds(column, a.shape[1])], sems.at[n]))
            copies[n].start()
    return copies


def near_kernel(near0, near1, near2, near3, weights, tok_t, grad_t, out, gate_grad, up_grad, down_grad, held, sems):
    width = near0.shape[1]
    pieces = [(near0, near2, place(0, 0, width))]
    copies = weight_grad_copies(pieces, tok_t, grad_t, (gate_grad, up_grad, down_grad), held, sems)
    out[...] = slot_part(near0, near2, weights, 0) + slot_part(near1, near3, weights, 1)
    for copy in copies:
        copy.wait()


def slot_kernel(before, far, weights, out):
    experts, slots, _ = out.shape
    total = before[...]
    for jy in range(2):
        total += slot_part(far.at[jy], far.at[2 + jy], weights, jy)
    for part in range(2):
        for j in range(experts // 2):
            start = (part * (experts // 2) + j) * slots
            out[(row_part() ^ part) * (experts // 2) + j] = total[start : start + slots].astype(BF16)


def weight_grad_kernel(near0, near1, near2, near3, far, tok_t, grad_t, *refs):
    gate_grad, up_grad, down_grad, prob_out, held, sems, prob_held, prob_sem = refs[3:]
    width = far.shape[2]
    pieces = [(near1, near3, place(0, 1, width))]
    pieces += [(far.at[jy], far.at[2 + jy], place(1, jy, width)) for jy in range(2)]
    copies = weight_grad_copies(pieces, tok_t, grad_t, (gate_grad, up_grad, down_grad), held, sems)
    tail = jnp.zeros((8, width), F32)
    for chunk in (near0, near1, near2, near3, far.at[0], far.at[1], far.at[2], far.at[3]):
        tail += chunk[...].astype(F32)[-8:]
    prob = jnp.broadcast_to(tail[0:1] + tail[1:2], (8, width))
    share = prob_out.shape[1]
    shift = lax.rem(width - lax.axis_index("fsdp") * share, width)
    prob_held[...] = pltpu.roll(prob, shift, 1)[:1, :share]
    copies.append(pltpu.make_async_copy(prob_held, prob_out, prob_sem))
    copies[-1].start()
    for copy in copies:
        copy.wait()


def token_grad_kernel(own, recv, onehot, out, held, sems):
    blocks = [own[...]] + [recv[j] for j in range(recv.shape[0])]
    slot_grad = jnp.concatenate([block.astype(F32) for block in blocks], axis=0).T.astype(BF16)
    count, _, width = held.shape
    copies = []
    for i in range(count):
        held[i] = dot(slot_grad, onehot[:, i * width : (i + 1) * width], (1, 0)).astype(BF16)
        copies.append(pltpu.make_async_copy(held.at[i], out.at[:, pl.ds(i * width, width)], sems.at[i]))
        copies[i].start()
    for copy in copies:
        copy.wait()


def local(tokens, out_grad, slot_rows, expert_counts, route_prob, w_gate, w_up, w_down):
    fsdp, experts = lax.axis_size("fsdp"), lax.axis_size("expert")
    steps = fsdp.bit_length() - 1
    token_count, features = tokens.shape
    _, _, slots = slot_rows.shape
    rows = experts * slots
    hidden = w_gate.shape[2]
    half, quarter = hidden // 2, hidden // 4
    def swap(x, *bits):
        mask = sum(1 << b for b in bits)
        return lax.ppermute(x, "fsdp", [(i, i ^ mask) for i in range(fsdp)])

    def to_expert(x):
        if experts == 2:
            return x[0], lax.ppermute(x[1], "expert", [(0, 1), (1, 0)])[None]
        moved = lax.all_to_all(x, "expert", split_axis=0, concat_axis=0, tiled=True)
        return moved[0], moved[1:]

    half_shape = jax.ShapeDtypeStruct((3, features, half), BF16)
    rows_out, onehot, far_weights = pl.pallas_call(
        gather_kernel,
        out_shape=(
            jax.ShapeDtypeStruct((experts, 2, slots, features), BF16),
            jax.ShapeDtypeStruct((rows, token_count), BF16),
            half_shape,
        ),
        in_specs=[HBM] * 6,
        out_specs=(VMEM,) * 3,
        scratch_shapes=[
            pltpu.SMEM((experts, slots), jnp.int32),
            pltpu.VMEM((features, token_count), BF16),
            pltpu.VMEM((features, token_count), BF16),
            pltpu.VMEM((rows, token_count), F32),
            pltpu.SemaphoreType.DMA((3,)),
            pltpu.SemaphoreType.DMA((3,)),
        ],
        compiler_params=PARAMS,
        name="gather_rows",
    )(*(in_hbm(x) for x in (slot_rows[0], tokens.T, out_grad.T, w_gate, w_up, w_down)))
    own, recv = to_expert(rows_out)
    if experts == 2:
        crossed = [(f * 2 + x, (f ^ 1) * 2 + 1 - x) for f in range(fsdp) for x in range(2)]
        other_recv = lax.ppermute(rows_out[1], ("fsdp", "expert"), crossed)[None]
    else:
        other_recv = swap(recv, 0)
    other_own = swap(own, 0)
    other_weights = swap(far_weights, 0)
    near_weights = pl.pallas_call(
        load_kernel,
        out_shape=half_shape,
        in_specs=[VMEM] + [HBM] * 3,
        out_specs=VMEM,
        scratch_shapes=[pltpu.SemaphoreType.DMA((3,))],
        compiler_params=PARAMS,
        cost_estimate=pl.CostEstimate(flops=0, bytes_accessed=6 * features * half, transcendentals=0),
        name="load_weights",
    )(own, *(in_hbm(w) for w in (w_gate, w_up, w_down)))
    kept = pl.pallas_call(
        partial_kernel,
        out_shape=jax.ShapeDtypeStruct((4, 3 * rows // 2, quarter), F32),
        in_specs=[VMEM] * 3,
        out_specs=VMEM,
        compiler_params=PARAMS,
        cost_estimate=pl.CostEstimate(
            flops=6 * rows * features * half, bytes_accessed=6 * features * half, transcendentals=0
        ),
        name="partial_sums",
    )(own, recv, near_weights)
    turned_shape = jax.ShapeDtypeStruct((features, rows), BF16)
    fact_shape = jax.ShapeDtypeStruct((rows // 2, 128), F32)
    diagonal_shape = jax.ShapeDtypeStruct((rows // 2, (rows + 127) // 128 * 128), F32)
    tok_t, grad_t, scale, live, diagonal = pl.pallas_call(
        rows_kernel,
        out_shape=(turned_shape, turned_shape, fact_shape, fact_shape, diagonal_shape),
        in_specs=[SMEM] + [VMEM] * 3,
        out_specs=(VMEM,) * 5,
        compiler_params=PARAMS,
        cost_estimate=pl.CostEstimate(flops=0, bytes_accessed=8 * features * rows, transcendentals=0),
        name="row_facts",
    )(expert_counts[0], own, recv, route_prob)
    coded_shape = jax.ShapeDtypeStruct((3 * rows // 2 + 8, quarter), F32)
    total, power, *sent = pl.pallas_call(
        add_kernel,
        out_shape=(
            jax.ShapeDtypeStruct((3 * rows // 2, quarter), F32),
            jax.ShapeDtypeStruct((8, quarter), F32),
        )
        + (coded_shape,) * 3,
        in_specs=[VMEM] * 4,
        out_specs=(VMEM,) * 5,
        scratch_shapes=[pltpu.VMEM(kept.shape, F32)],
        compiler_params=PARAMS,
        name="add_other_core",
    )(kept, other_own, other_recv, other_weights)
    arrived = [swap(x.astype(F16), *bits) for x, bits in zip(sent, ((1,), (2,), (1, 2)))]
    for x in arrived:
        chunk, its_power = decoded(x)
        total, power = total + chunk, jnp.maximum(power, its_power)
    power += 2.0
    for b in range(3, steps):
        arrived, its_power = decoded(swap(coded(total, power).astype(F16), b))
        if b < steps - 1:
            total, power = total + arrived, jnp.maximum(power, its_power) + 1.0
    acts = pl.pallas_call(
        hidden_kernel,
        out_shape=jax.ShapeDtypeStruct((3 * rows // 2 + 8, quarter), BF16),
        in_specs=[VMEM] * 5,
        out_specs=VMEM,
        compiler_params=PARAMS,
        name="hidden",
    )(scale, live, diagonal, total, arrived)
    near = [acts, swap(acts, 1), swap(acts, 2), swap(acts, 1, 2)]
    far = swap(jnp.stack(near), 0)

    grad_shape = jax.ShapeDtypeStruct((1, features, hidden), F32)

    def held(count):
        return [pltpu.VMEM((count, features, quarter), F32), pltpu.SemaphoreType.DMA((count,))]

    near_slot, *grads = pl.pallas_call(
        near_kernel,
        out_shape=(jax.ShapeDtypeStruct((rows, features), F32),) + (grad_shape,) * 3,
        in_specs=[VMEM] * 7,
        out_specs=(VMEM,) + (HBM,) * 3,
        scratch_shapes=held(3),
        compiler_params=PARAMS,
        cost_estimate=pl.CostEstimate(
            flops=4 * rows * features * hidden, bytes_accessed=3 * features * hidden, transcendentals=0
        ),
        name="near_piece",
    )(*near, near_weights, tok_t, grad_t)
    slot_grad = pl.pallas_call(
        slot_kernel,
        out_shape=jax.ShapeDtypeStruct((experts, slots, features), BF16),
        in_specs=[VMEM] * 3,
        out_specs=VMEM,
        compiler_params=PARAMS,
        name="slot_grad",
    )(near_slot, far, far_weights)
    slot_own, slot_recv = to_expert(slot_grad)
    gate_grad, up_grad, down_grad, prob_grad = pl.pallas_call(
        weight_grad_kernel,
        out_shape=(grad_shape,) * 3 + (jax.ShapeDtypeStruct((1, rows // fsdp), F32),),
        in_specs=[VMEM] * 7 + [HBM] * 3,
        out_specs=(HBM,) * 4,
        scratch_shapes=held(9) + [pltpu.VMEM((1, rows // fsdp), F32), pltpu.SemaphoreType.DMA],
        input_output_aliases={7 + i: i for i in range(3)},
        compiler_params=PARAMS,
        cost_estimate=pl.CostEstimate(
            flops=4 * rows * features * hidden, bytes_accessed=9 * features * hidden, transcendentals=0
        ),
        name="weight_grads",
    )(*near, far, tok_t, grad_t, *grads)

    token_grad = pl.pallas_call(
        token_grad_kernel,
        out_shape=jax.ShapeDtypeStruct((features, token_count), BF16),
        in_specs=[VMEM] * 3,
        out_specs=HBM,
        scratch_shapes=[pltpu.VMEM((4, features, token_count // 4), BF16), pltpu.SemaphoreType.DMA((4,))],
        compiler_params=PARAMS,
        name="token_grad",
    )(slot_own, slot_recv, onehot).T
    return (token_grad, gate_grad, up_grad, down_grad, prob_grad)


def solution(mesh):
    return jax.shard_map(
        local,
        mesh=mesh,
        in_specs=(
            P("expert", "fsdp"),
            P("expert", "fsdp"),
            P("expert", None, None),
            P("expert", None),
            P("expert", None),
            P("expert", "fsdp", None),
            P("expert", "fsdp", None),
            P("expert", "fsdp", None),
        ),
        out_specs=(
            P("expert", "fsdp"),
            P("expert", "fsdp", None),
            P("expert", "fsdp", None),
            P("expert", "fsdp", None),
            P("expert", "fsdp"),
        ),
        check_vma=False,
    )
```

```python
import functools

import jax
import jax.numpy as jnp
from jax import lax
from jax.experimental import pallas as pl
from jax.experimental.pallas import tpu as pltpu
from jax.sharding import PartitionSpec as P

BF16 = jnp.bfloat16
F32 = jnp.float32
F16 = jnp.float16
VMEM = pl.BlockSpec(memory_space=pltpu.VMEM)
HBM = pl.BlockSpec(memory_space=pltpu.HBM)
SMEM = pl.BlockSpec(memory_space=pltpu.SMEM)
PARAMS = pltpu.CompilerParams(vmem_limit_bytes=40 * 2**20)

def in_hbm(x):
    return pltpu.with_memory_space_constraint(x, pltpu.HBM)


def dot(a, b, contract):
    return lax.dot_general(a, b, ((contract[0:1], contract[1:2]), ((), ())), preferred_element_type=F32)


def place(side, jy, width):
    me = lax.axis_index("fsdp")
    half = (me & 1) ^ side
    return pl.multiple_of((half * 2 + (((me >> 1) & 1) ^ jy)) * width, 128)


def place_in_half(jy, width):
    return pl.multiple_of((((lax.axis_index("fsdp") >> 1) & 1) ^ jy) * width, 128)


def half_copies(side, weights, to, sems):
    width = to.shape[2]
    at = pl.ds(pl.multiple_of(((lax.axis_index("fsdp") & 1) ^ side) * width, 128), width)
    return [pltpu.make_async_copy(w.at[0, :, at], to.at[i], sems.at[i]) for i, w in enumerate(weights)]


def row_part():
    return (lax.axis_index("fsdp") >> 2) & 1


def first_expert(experts):
    return lax.axis_index("expert") if experts == 2 else 0


def gather_kernel(slot_rows_hbm, tokens_hbm, grads_hbm, *refs):
    weights, (rows_out, onehot_out, far_out, slot_rows, tokens_t, grads_t, onehot_f, sems, far_sems) = refs[:3], refs[3:]
    copies = [
        pltpu.make_async_copy(source, to, sems.at[i])
        for i, (source, to) in enumerate(((slot_rows_hbm, slot_rows), (tokens_hbm, tokens_t), (grads_hbm, grads_t)))
    ]
    far_copies = half_copies(1, weights, far_out, far_sems)
    for copy in copies + far_copies:
        copy.start()
    experts, slots = slot_rows.shape
    count = tokens_t.shape[1]
    first = first_expert(experts)
    lane = lax.broadcasted_iota(jnp.int32, (8, count), 1)
    sub = lax.broadcasted_iota(jnp.int32, (8, count), 0)
    copies[0].wait()
    for j in range(experts):
        expert = lax.rem(first + j, experts)
        for base in range(0, slots, 8):
            picked = jnp.zeros((8, count), jnp.int32)
            for r in range(8):
                picked = jnp.where(sub == r, slot_rows[expert, base + r], picked)
            onehot_f[pl.ds(j * slots + base, 8), :] = (picked == lane).astype(F32)
    onehot = onehot_f[...].astype(BF16)
    onehot_out[...] = onehot
    for kind, source in enumerate((tokens_t, grads_t)):
        copies[1 + kind].wait()
        rows = dot(onehot, source[...], (1, 1))
        for j in range(experts):
            rows_out[j, kind] = rows[j * slots : (j + 1) * slots].astype(BF16)
    for copy in far_copies:
        copy.wait()


def load_kernel(after, w_gate, w_up, w_down, out, sems):
    del after
    copies = half_copies(0, (w_gate, w_up, w_down), out, sems)
    for copy in copies:
        copy.start()
    for copy in copies:
        copy.wait()


def stacked_rows(own, recv, kind):
    blocks = [own[kind]] + [recv[j, kind] for j in range(recv.shape[0])]
    return jnp.concatenate([block.astype(F32) for block in blocks], axis=0)


def partial_sums(own, recv, weights, width, jy, q):
    rows = stacked_rows(own, recv, q // 2).astype(BF16)
    return dot(rows, weights[q, :, pl.ds(place_in_half(jy, width), width)], (1, 0))


def partial_kernel(own, recv, weights, out):
    chunk_rows, width = out.shape[1] // 3, out.shape[2]
    for jy in range(2):
        for q in range(3):
            sums = partial_sums(own, recv, weights, width, jy, q)
            for part in range(2):
                chunk = (row_part() ^ part) * 2 + jy
                out[chunk, pl.ds(q * chunk_rows, chunk_rows), :] = sums[part * chunk_rows : (part + 1) * chunk_rows]


def rows_kernel(counts, own, recv, prob, tok_t, grad_t, scale_out, live_out, diagonal_out):
    part0 = row_part()
    rows, lanes = diagonal_out.shape
    for to, x in ((tok_t, stacked_rows(own, recv, 0)), (grad_t, stacked_rows(own, recv, 1))):
        low, high = x[:rows], x[rows:]
        near, far = jnp.where(part0 == 0, low, high), jnp.where(part0 == 0, high, low)
        to[...] = jnp.concatenate([near, far], axis=0).T.astype(BF16)
    experts = counts.shape[0]
    slots = 2 * rows // experts
    first = first_expert(experts)
    row = lax.broadcasted_iota(jnp.int32, (rows, lanes), 0) + part0 * rows
    lane = lax.broadcasted_iota(jnp.int32, (rows, lanes), 1)
    slot, home, live_count = row, row, row
    for j in range(experts):
        source = lax.rem(first + j, experts)
        inside = (row >= j * slots) & (row < (j + 1) * slots)
        slot = jnp.where(inside, row - j * slots, slot)
        home = jnp.where(inside, source * slots + row - j * slots, home)
        live_count = jnp.where(inside, counts[source], live_count)
    live = (slot < live_count).astype(F32)
    diagonal = lane == home
    probs = jnp.concatenate([prob[...], jnp.zeros((1, lanes - 2 * rows), F32)], axis=1)
    row_prob = jnp.sum(jnp.where(diagonal, probs, 0.0), axis=1, keepdims=True)
    scale_out[...] = row_prob * live[:, :128]
    live_out[...] = live[:, :128]
    diagonal_out[...] = diagonal.astype(F32)


def add_kernel(kept, own, recv, weights, first, power_out, *refs):
    outs, summed = refs[:-1], refs[-1]
    partial_kernel(own, recv, weights, summed)
    rows = first.shape[0] // 3
    width = first.shape[1]
    chunks = [kept[j] + summed[j] for j in range(4)]
    first[...] = chunks[0]
    powers = []
    for q in range(3):
        most = functools.reduce(jnp.maximum, [jnp.abs(x[q * rows : (q + 1) * rows]) for x in chunks])
        most = jnp.max(jnp.max(most, axis=0, keepdims=True), axis=1, keepdims=True)
        most = jnp.maximum(jnp.broadcast_to(most, (1, width)), 1e-30)
        powers.append(jnp.ceil(jnp.log2(most)) - 14.0)
    power_out[...] = jnp.concatenate(powers + [jnp.zeros((5, width), F32)], axis=0)
    for x, out in zip(chunks[1:], outs):
        for q in range(3):
            out[pl.ds(q * rows, rows), :] = x[q * rows : (q + 1) * rows] * jnp.exp2(-powers[q])
        out[pl.ds(3 * rows, 8), :] = power_out[...]


def scaled(x, power):
    rows = x.shape[0] // 3
    return (x.reshape(3, rows, -1) * jnp.exp2(power[:3])[:, None]).reshape(x.shape)


def coded(x, power):
    return jnp.concatenate([scaled(x, -power), power], axis=0)


def decoded(x):
    x = x.astype(F32)
    return scaled(x[:-8], x[-8:]), x[-8:]


def hidden_kernel(scale, live, diagonal, sums, recv, out):
    rows = sums.shape[0] // 3
    width = sums.shape[1]
    total = sums[...] + recv[...]
    gate, up, down = total[:rows], total[rows : 2 * rows], total[2 * rows :]
    row_scale = jnp.concatenate([scale[...]] * (width // 128), axis=1)
    sigmoid = jax.nn.sigmoid(gate)
    silu = gate * sigmoid
    hidden = (silu * up).astype(BF16).astype(F32)
    hidden_grad = down * row_scale
    gate_act_grad = hidden_grad * up * sigmoid * (1.0 + gate * (1.0 - sigmoid))
    prob_grad = live[:, :1] * jnp.sum(hidden * down, axis=1, keepdims=True)
    prob_row = jnp.sum(diagonal[...] * prob_grad, axis=0, keepdims=True)
    high = prob_row.astype(BF16).astype(F32)
    tail = jnp.concatenate([high, prob_row - high, jnp.zeros((6, prob_row.shape[1]), F32)], axis=0)
    tail = jnp.concatenate([tail, jnp.zeros((8, width - prob_row.shape[1]), F32)], axis=1)
    out[...] = jnp.concatenate([hidden * row_scale, gate_act_grad, hidden_grad * silu, tail], axis=0).astype(BF16)


def parts(a, b):
    a, b = a[...].astype(F32), b[...].astype(F32)
    rows = (a.shape[0] - 8) // 3
    both = [jnp.concatenate([a[q * rows : (q + 1) * rows], b[q * rows : (q + 1) * rows]], axis=0) for q in range(3)]
    return [x.astype(BF16) for x in both]


def slot_part(a, b, weights, jy):
    _, gate_act_grad, up_act_grad = parts(a, b)
    at = pl.ds(place_in_half(jy, a.shape[1]), a.shape[1])
    return dot(gate_act_grad, weights[0, :, at], (1, 1)) + dot(up_act_grad, weights[1, :, at], (1, 1))


def weight_grad_copies(pieces, tok_t, grad_t, outs, held, sems):
    copies = []
    for a, b, column in pieces:
        down, gate, up = parts(a, b)
        for x, y, out in ((tok_t, gate, outs[0]), (tok_t, up, outs[1]), (grad_t, down, outs[2])):
            n = len(copies)
            held[n] = dot(x[...], y, (1, 0))
            copies.append(pltpu.make_async_copy(held.at[n], out.at[0, :, pl.ds(column, a.shape[1])], sems.at[n]))
            copies[n].start()
    return copies


def near_kernel(near0, near1, near2, near3, weights, tok_t, grad_t, out, gate_grad, up_grad, down_grad, held, sems):
    width = near0.shape[1]
    pieces = [(near0, near2, place(0, 0, width))]
    copies = weight_grad_copies(pieces, tok_t, grad_t, (gate_grad, up_grad, down_grad), held, sems)
    out[...] = slot_part(near0, near2, weights, 0) + slot_part(near1, near3, weights, 1)
    for copy in copies:
        copy.wait()


def slot_kernel(before, far, weights, out):
    experts, slots, _ = out.shape
    total = before[...]
    for jy in range(2):
        total += slot_part(far.at[jy], far.at[2 + jy], weights, jy)
    for part in range(2):
        for j in range(experts // 2):
            start = (part * (experts // 2) + j) * slots
            out[(row_part() ^ part) * (experts // 2) + j] = total[start : start + slots].astype(BF16)


def weight_grad_kernel(near0, near1, near2, near3, far, tok_t, grad_t, *refs):
    gate_grad, up_grad, down_grad, prob_out, held, sems, prob_held, prob_sem = refs[3:]
    width = far.shape[2]
    pieces = [(near1, near3, place(0, 1, width))]
    pieces += [(far.at[jy], far.at[2 + jy], place(1, jy, width)) for jy in range(2)]
    copies = weight_grad_copies(pieces, tok_t, grad_t, (gate_grad, up_grad, down_grad), held, sems)
    tail = jnp.zeros((8, width), F32)
    for chunk in (near0, near1, near2, near3, far.at[0], far.at[1], far.at[2], far.at[3]):
        tail += chunk[...].astype(F32)[-8:]
    prob = jnp.broadcast_to(tail[0:1] + tail[1:2], (8, width))
    share = prob_out.shape[1]
    shift = lax.rem(width - lax.axis_index("fsdp") * share, width)
    prob_held[...] = pltpu.roll(prob, shift, 1)[:1, :share]
    copies.append(pltpu.make_async_copy(prob_held, prob_out, prob_sem))
    copies[-1].start()
    for copy in copies:
        copy.wait()


def token_grad_kernel(own, recv, onehot, out, held, sems):
    blocks = [own[...]] + [recv[j] for j in range(recv.shape[0])]
    slot_grad = jnp.concatenate([block.astype(F32) for block in blocks], axis=0).T.astype(BF16)
    copies = []
    step = out.shape[0] // 5
    for i in range(5):
        rows = pl.ds(i * step, step)
        held[rows, :] = dot(slot_grad[i * step : (i + 1) * step], onehot[...], (1, 0)).astype(BF16)
        copies.append(pltpu.make_async_copy(held.at[rows], out.at[rows], sems.at[i]))
        copies[i].start()
    for copy in copies:
        copy.wait()


def local(tokens, out_grad, slot_rows, expert_counts, route_prob, w_gate, w_up, w_down):
    fsdp, experts = lax.axis_size("fsdp"), lax.axis_size("expert")
    steps = fsdp.bit_length() - 1
    token_count, features = tokens.shape
    _, _, slots = slot_rows.shape
    rows = experts * slots
    hidden = w_gate.shape[2]
    half, quarter = hidden // 2, hidden // 4
    def swap(x, *bits):
        mask = sum(1 << b for b in bits)
        return lax.ppermute(x, "fsdp", [(i, i ^ mask) for i in range(fsdp)])

    def to_expert(x):
        if experts == 2:
            return x[0], lax.ppermute(x[1], "expert", [(0, 1), (1, 0)])[None]
        moved = lax.all_to_all(x, "expert", split_axis=0, concat_axis=0, tiled=True)
        return moved[0], moved[1:]

    half_shape = jax.ShapeDtypeStruct((3, features, half), BF16)
    rows_out, onehot, far_weights = pl.pallas_call(
        gather_kernel,
        out_shape=(
            jax.ShapeDtypeStruct((experts, 2, slots, features), BF16),
            jax.ShapeDtypeStruct((rows, token_count), BF16),
            half_shape,
        ),
        in_specs=[HBM] * 6,
        out_specs=(VMEM,) * 3,
        scratch_shapes=[
            pltpu.SMEM((experts, slots), jnp.int32),
            pltpu.VMEM((features, token_count), BF16),
            pltpu.VMEM((features, token_count), BF16),
            pltpu.VMEM((rows, token_count), F32),
            pltpu.SemaphoreType.DMA((3,)),
            pltpu.SemaphoreType.DMA((3,)),
        ],
        compiler_params=PARAMS,
        name="gather_rows",
    )(*(in_hbm(x) for x in (slot_rows[0], tokens.T, out_grad.T, w_gate, w_up, w_down)))
    own, recv = to_expert(rows_out)
    if experts == 2:
        crossed = [(f * 2 + x, (f ^ 1) * 2 + 1 - x) for f in range(fsdp) for x in range(2)]
        other_recv = lax.ppermute(rows_out[1], ("fsdp", "expert"), crossed)[None]
    else:
        other_recv = swap(recv, 0)
    other_own = swap(own, 0)
    other_weights = swap(far_weights, 0)
    near_weights = pl.pallas_call(
        load_kernel,
        out_shape=half_shape,
        in_specs=[VMEM] + [HBM] * 3,
        out_specs=VMEM,
        scratch_shapes=[pltpu.SemaphoreType.DMA((3,))],
        compiler_params=PARAMS,
        cost_estimate=pl.CostEstimate(flops=0, bytes_accessed=6 * features * half, transcendentals=0),
        name="load_weights",
    )(own, *(in_hbm(w) for w in (w_gate, w_up, w_down)))
    kept = pl.pallas_call(
        partial_kernel,
        out_shape=jax.ShapeDtypeStruct((4, 3 * rows // 2, quarter), F32),
        in_specs=[VMEM] * 3,
        out_specs=VMEM,
        compiler_params=PARAMS,
        cost_estimate=pl.CostEstimate(
            flops=6 * rows * features * half, bytes_accessed=6 * features * half, transcendentals=0
        ),
        name="partial_sums",
    )(own, recv, near_weights)
    turned_shape = jax.ShapeDtypeStruct((features, rows), BF16)
    fact_shape = jax.ShapeDtypeStruct((rows // 2, 128), F32)
    diagonal_shape = jax.ShapeDtypeStruct((rows // 2, (rows + 127) // 128 * 128), F32)
    tok_t, grad_t, scale, live, diagonal = pl.pallas_call(
        rows_kernel,
        out_shape=(turned_shape, turned_shape, fact_shape, fact_shape, diagonal_shape),
        in_specs=[SMEM] + [VMEM] * 3,
        out_specs=(VMEM,) * 5,
        compiler_params=PARAMS,
        cost_estimate=pl.CostEstimate(flops=0, bytes_accessed=8 * features * rows, transcendentals=0),
        name="row_facts",
    )(expert_counts[0], own, recv, route_prob)
    coded_shape = jax.ShapeDtypeStruct((3 * rows // 2 + 8, quarter), F32)
    total, power, *sent = pl.pallas_call(
        add_kernel,
        out_shape=(
            jax.ShapeDtypeStruct((3 * rows // 2, quarter), F32),
            jax.ShapeDtypeStruct((8, quarter), F32),
        )
        + (coded_shape,) * 3,
        in_specs=[VMEM] * 4,
        out_specs=(VMEM,) * 5,
        scratch_shapes=[pltpu.VMEM(kept.shape, F32)],
        compiler_params=PARAMS,
        name="add_other_core",
    )(kept, other_own, other_recv, other_weights)
    arrived = [swap(x.astype(F16), *bits) for x, bits in zip(sent, ((1,), (2,), (1, 2)))]
    for x in arrived:
        chunk, its_power = decoded(x)
        total, power = total + chunk, jnp.maximum(power, its_power)
    power += 2.0
    for b in range(3, steps):
        arrived, its_power = decoded(swap(coded(total, power).astype(F16), b))
        if b < steps - 1:
            total, power = total + arrived, jnp.maximum(power, its_power) + 1.0
    acts = pl.pallas_call(
        hidden_kernel,
        out_shape=jax.ShapeDtypeStruct((3 * rows // 2 + 8, quarter), BF16),
        in_specs=[VMEM] * 5,
        out_specs=VMEM,
        compiler_params=PARAMS,
        name="hidden",
    )(scale, live, diagonal, total, arrived)
    near = [acts, swap(acts, 1), swap(acts, 2), swap(acts, 1, 2)]
    far = swap(jnp.stack(near), 0)

    grad_shape = jax.ShapeDtypeStruct((1, features, hidden), F32)

    def held(count):
        return [pltpu.VMEM((count, features, quarter), F32), pltpu.SemaphoreType.DMA((count,))]

    near_slot, *grads = pl.pallas_call(
        near_kernel,
        out_shape=(jax.ShapeDtypeStruct((rows, features), F32),) + (grad_shape,) * 3,
        in_specs=[VMEM] * 7,
        out_specs=(VMEM,) + (HBM,) * 3,
        scratch_shapes=held(3),
        compiler_params=PARAMS,
        cost_estimate=pl.CostEstimate(
            flops=4 * rows * features * hidden, bytes_accessed=3 * features * hidden, transcendentals=0
        ),
        name="near_piece",
    )(*near, near_weights, tok_t, grad_t)
    slot_grad = pl.pallas_call(
        slot_kernel,
        out_shape=jax.ShapeDtypeStruct((experts, slots, features), BF16),
        in_specs=[VMEM] * 3,
        out_specs=VMEM,
        compiler_params=PARAMS,
        name="slot_grad",
    )(near_slot, far, far_weights)
    slot_own, slot_recv = to_expert(slot_grad)
    gate_grad, up_grad, down_grad, prob_grad = pl.pallas_call(
        weight_grad_kernel,
        out_shape=(grad_shape,) * 3 + (jax.ShapeDtypeStruct((1, rows // fsdp), F32),),
        in_specs=[VMEM] * 7 + [HBM] * 3,
        out_specs=(HBM,) * 4,
        scratch_shapes=held(9) + [pltpu.VMEM((1, rows // fsdp), F32), pltpu.SemaphoreType.DMA],
        input_output_aliases={7 + i: i for i in range(3)},
        compiler_params=PARAMS,
        cost_estimate=pl.CostEstimate(
            flops=4 * rows * features * hidden, bytes_accessed=9 * features * hidden, transcendentals=0
        ),
        name="weight_grads",
    )(*near, far, tok_t, grad_t, *grads)

    token_grad = pl.pallas_call(
        token_grad_kernel,
        out_shape=jax.ShapeDtypeStruct((features, token_count), BF16),
        in_specs=[VMEM] * 3,
        out_specs=HBM,
        scratch_shapes=[pltpu.VMEM((features, token_count), BF16), pltpu.SemaphoreType.DMA((5,))],
        compiler_params=PARAMS,
        name="token_grad",
    )(slot_own, slot_recv, onehot).T
    return (token_grad, gate_grad, up_grad, down_grad, prob_grad)


def solution(mesh):
    return jax.shard_map(
        local,
        mesh=mesh,
        in_specs=(
            P("expert", "fsdp"),
            P("expert", "fsdp"),
            P("expert", None, None),
            P("expert", None),
            P("expert", None),
            P("expert", "fsdp", None),
            P("expert", "fsdp", None),
            P("expert", "fsdp", None),
        ),
        out_specs=(
            P("expert", "fsdp"),
            P("expert", "fsdp", None),
            P("expert", "fsdp", None),
            P("expert", "fsdp", None),
            P("expert", "fsdp"),
        ),
        check_vma=False,
    )
```

```python
import functools

import jax
import jax.numpy as jnp
from jax import lax
from jax.experimental import pallas as pl
from jax.experimental.pallas import tpu as pltpu
from jax.sharding import PartitionSpec as P

BF16 = jnp.bfloat16
F32 = jnp.float32
F16 = jnp.float16
VMEM = pl.BlockSpec(memory_space=pltpu.VMEM)
HBM = pl.BlockSpec(memory_space=pltpu.HBM)
SMEM = pl.BlockSpec(memory_space=pltpu.SMEM)
PARAMS = pltpu.CompilerParams(vmem_limit_bytes=40 * 2**20)

def in_hbm(x):
    return pltpu.with_memory_space_constraint(x, pltpu.HBM)


def dot(a, b, contract):
    return lax.dot_general(a, b, ((contract[0:1], contract[1:2]), ((), ())), preferred_element_type=F32)


def place(side, jy, width):
    me = lax.axis_index("fsdp")
    half = (me & 1) ^ side
    return pl.multiple_of((half * 2 + (((me >> 1) & 1) ^ jy)) * width, 128)


def place_in_half(jy, width):
    return pl.multiple_of((((lax.axis_index("fsdp") >> 1) & 1) ^ jy) * width, 128)


def half_copies(side, weights, to, sems):
    width = to.shape[2]
    at = pl.ds(pl.multiple_of(((lax.axis_index("fsdp") & 1) ^ side) * width, 128), width)
    return [pltpu.make_async_copy(w.at[0, :, at], to.at[i], sems.at[i]) for i, w in enumerate(weights)]


def row_part():
    return (lax.axis_index("fsdp") >> 2) & 1


def first_expert(experts):
    return lax.axis_index("expert") if experts == 2 else 0


def gather_kernel(slot_rows_hbm, tokens_hbm, grads_hbm, *refs):
    weights, (rows_out, onehot_out, far_out, slot_rows, tokens_t, grads_t, onehot_f, sems, far_sems) = refs[:3], refs[3:]
    copies = [
        pltpu.make_async_copy(source, to, sems.at[i])
        for i, (source, to) in enumerate(((slot_rows_hbm, slot_rows), (tokens_hbm, tokens_t), (grads_hbm, grads_t)))
    ]
    far_copies = half_copies(1, weights, far_out, far_sems)
    for copy in copies + far_copies:
        copy.start()
    experts, slots = slot_rows.shape
    count = tokens_t.shape[1]
    first = first_expert(experts)
    lane = lax.broadcasted_iota(jnp.int32, (8, count), 1)
    sub = lax.broadcasted_iota(jnp.int32, (8, count), 0)
    copies[0].wait()
    for j in range(experts):
        expert = lax.rem(first + j, experts)
        for base in range(0, slots, 8):
            picked = jnp.zeros((8, count), jnp.int32)
            for r in range(8):
                picked = jnp.where(sub == r, slot_rows[expert, base + r], picked)
            onehot_f[pl.ds(j * slots + base, 8), :] = (picked == lane).astype(F32)
    onehot = onehot_f[...].astype(BF16)
    onehot_out[...] = onehot
    for kind, source in enumerate((tokens_t, grads_t)):
        copies[1 + kind].wait()
        rows = dot(onehot, source[...], (1, 1))
        for j in range(experts):
            rows_out[j, kind] = rows[j * slots : (j + 1) * slots].astype(BF16)
    for copy in far_copies:
        copy.wait()


def load_kernel(after, w_gate, w_up, w_down, out, sems):
    del after
    copies = half_copies(0, (w_gate, w_up, w_down), out, sems)
    for copy in copies:
        copy.start()
    for copy in copies:
        copy.wait()


def stacked_rows(own, recv, kind):
    blocks = [own[kind]] + [recv[j, kind] for j in range(recv.shape[0])]
    return jnp.concatenate([block.astype(F32) for block in blocks], axis=0)


def partial_sums(own, recv, weights, width, jy, q):
    rows = stacked_rows(own, recv, q // 2).astype(BF16)
    return dot(rows, weights[q, :, pl.ds(place_in_half(jy, width), width)], (1, 0))


def partial_kernel(own, recv, weights, out):
    chunk_rows, width = out.shape[1] // 3, out.shape[2]
    for jy in range(2):
        for q in range(3):
            sums = partial_sums(own, recv, weights, width, jy, q)
            for part in range(2):
                chunk = (row_part() ^ part) * 2 + jy
                out[chunk, pl.ds(q * chunk_rows, chunk_rows), :] = sums[part * chunk_rows : (part + 1) * chunk_rows]


def rows_kernel(counts, own, recv, prob, tok_t, grad_t, scale_out, live_out, diagonal_out):
    part0 = row_part()
    rows, lanes = diagonal_out.shape
    for to, x in ((tok_t, stacked_rows(own, recv, 0)), (grad_t, stacked_rows(own, recv, 1))):
        low, high = x[:rows], x[rows:]
        near, far = jnp.where(part0 == 0, low, high), jnp.where(part0 == 0, high, low)
        to[...] = jnp.concatenate([near, far], axis=0).T.astype(BF16)
    experts = counts.shape[0]
    slots = 2 * rows // experts
    first = first_expert(experts)
    row = lax.broadcasted_iota(jnp.int32, (rows, lanes), 0) + part0 * rows
    lane = lax.broadcasted_iota(jnp.int32, (rows, lanes), 1)
    slot, home, live_count = row, row, row
    for j in range(experts):
        source = lax.rem(first + j, experts)
        inside = (row >= j * slots) & (row < (j + 1) * slots)
        slot = jnp.where(inside, row - j * slots, slot)
        home = jnp.where(inside, source * slots + row - j * slots, home)
        live_count = jnp.where(inside, counts[source], live_count)
    live = (slot < live_count).astype(F32)
    diagonal = lane == home
    probs = jnp.concatenate([prob[...], jnp.zeros((1, lanes - 2 * rows), F32)], axis=1)
    row_prob = jnp.sum(jnp.where(diagonal, probs, 0.0), axis=1, keepdims=True)
    scale_out[...] = row_prob * live[:, :128]
    live_out[...] = live[:, :128]
    diagonal_out[...] = diagonal.astype(F32)


def add_kernel(kept, own, recv, weights, first, power_out, *refs):
    outs, summed = refs[:-1], refs[-1]
    partial_kernel(own, recv, weights, summed)
    rows = first.shape[0] // 3
    width = first.shape[1]
    chunks = [kept[j] + summed[j] for j in range(4)]
    first[...] = chunks[0]
    powers = []
    for q in range(3):
        most = functools.reduce(jnp.maximum, [jnp.abs(x[q * rows : (q + 1) * rows]) for x in chunks])
        most = jnp.maximum(jnp.max(most, axis=0, keepdims=True), 1e-30)
        powers.append(jnp.ceil(jnp.log2(most)) - 14.0)
    power_out[...] = jnp.concatenate(powers + [jnp.zeros((5, width), F32)], axis=0)
    for x, out in zip(chunks[1:], outs):
        for q in range(3):
            out[pl.ds(q * rows, rows), :] = x[q * rows : (q + 1) * rows] * jnp.exp2(-powers[q])
        out[pl.ds(3 * rows, 8), :] = power_out[...]


def scaled(x, power):
    rows = x.shape[0] // 3
    return (x.reshape(3, rows, -1) * jnp.exp2(power[:3])[:, None]).reshape(x.shape)


def coded(x, power):
    return jnp.concatenate([scaled(x, -power), power], axis=0)


def decoded(x):
    x = x.astype(F32)
    return scaled(x[:-8], x[-8:]), x[-8:]


def hidden_kernel(scale, live, diagonal, sums, recv, out):
    rows = sums.shape[0] // 3
    width = sums.shape[1]
    total = sums[...] + recv[...]
    gate, up, down = total[:rows], total[rows : 2 * rows], total[2 * rows :]
    row_scale = jnp.concatenate([scale[...]] * (width // 128), axis=1)
    sigmoid = jax.nn.sigmoid(gate)
    silu = gate * sigmoid
    hidden = (silu * up).astype(BF16).astype(F32)
    hidden_grad = down * row_scale
    gate_act_grad = hidden_grad * up * sigmoid * (1.0 + gate * (1.0 - sigmoid))
    prob_grad = live[:, :1] * jnp.sum(hidden * down, axis=1, keepdims=True)
    prob_row = jnp.sum(diagonal[...] * prob_grad, axis=0, keepdims=True)
    high = prob_row.astype(BF16).astype(F32)
    tail = jnp.concatenate([high, prob_row - high, jnp.zeros((6, prob_row.shape[1]), F32)], axis=0)
    tail = jnp.concatenate([tail, jnp.zeros((8, width - prob_row.shape[1]), F32)], axis=1)
    out[...] = jnp.concatenate([hidden * row_scale, gate_act_grad, hidden_grad * silu, tail], axis=0).astype(BF16)


def parts(a, b):
    a, b = a[...].astype(F32), b[...].astype(F32)
    rows = (a.shape[0] - 8) // 3
    both = [jnp.concatenate([a[q * rows : (q + 1) * rows], b[q * rows : (q + 1) * rows]], axis=0) for q in range(3)]
    return [x.astype(BF16) for x in both]


def slot_part(a, b, weights, jy):
    _, gate_act_grad, up_act_grad = parts(a, b)
    at = pl.ds(place_in_half(jy, a.shape[1]), a.shape[1])
    return dot(gate_act_grad, weights[0, :, at], (1, 1)) + dot(up_act_grad, weights[1, :, at], (1, 1))


def weight_grad_copies(pieces, tok_t, grad_t, outs, held, sems):
    copies = []
    for a, b, column in pieces:
        down, gate, up = parts(a, b)
        for x, y, out in ((tok_t, gate, outs[0]), (tok_t, up, outs[1]), (grad_t, down, outs[2])):
            n = len(copies)
            held[n] = dot(x[...], y, (1, 0))
            copies.append(pltpu.make_async_copy(held.at[n], out.at[0, :, pl.ds(column, a.shape[1])], sems.at[n]))
            copies[n].start()
    return copies


def near_kernel(near0, near1, near2, near3, weights, tok_t, grad_t, out, gate_grad, up_grad, down_grad, held, sems):
    width = near0.shape[1]
    pieces = [(near0, near2, place(0, 0, width))]
    copies = weight_grad_copies(pieces, tok_t, grad_t, (gate_grad, up_grad, down_grad), held, sems)
    out[...] = slot_part(near0, near2, weights, 0) + slot_part(near1, near3, weights, 1)
    for copy in copies:
        copy.wait()


def slot_kernel(before, far, weights, out):
    experts, slots, _ = out.shape
    total = before[...]
    for jy in range(2):
        total += slot_part(far.at[jy], far.at[2 + jy], weights, jy)
    for part in range(2):
        for j in range(experts // 2):
            start = (part * (experts // 2) + j) * slots
            out[(row_part() ^ part) * (experts // 2) + j] = total[start : start + slots].astype(BF16)


def weight_grad_kernel(near0, near1, near2, near3, far, tok_t, grad_t, *refs):
    gate_grad, up_grad, down_grad, prob_out, held, sems, prob_held, prob_sem = refs[3:]
    width = far.shape[2]
    pieces = [(near1, near3, place(0, 1, width))]
    pieces += [(far.at[jy], far.at[2 + jy], place(1, jy, width)) for jy in range(2)]
    copies = weight_grad_copies(pieces, tok_t, grad_t, (gate_grad, up_grad, down_grad), held, sems)
    tail = jnp.zeros((8, width), F32)
    for chunk in (near0, near1, near2, near3, far.at[0], far.at[1], far.at[2], far.at[3]):
        tail += chunk[...].astype(F32)[-8:]
    prob = jnp.broadcast_to(tail[0:1] + tail[1:2], (8, width))
    share = prob_out.shape[1]
    shift = lax.rem(width - lax.axis_index("fsdp") * share, width)
    prob_held[...] = pltpu.roll(prob, shift, 1)[:1, :share]
    copies.append(pltpu.make_async_copy(prob_held, prob_out, prob_sem))
    copies[-1].start()
    for copy in copies:
        copy.wait()


def token_grad_kernel(own, recv, onehot, out, held, sems):
    blocks = [own[...]] + [recv[j] for j in range(recv.shape[0])]
    slot_grad = jnp.concatenate([block.astype(F32) for block in blocks], axis=0).T.astype(BF16)
    copies = []
    step = out.shape[0] // 5
    for i in range(5):
        rows = pl.ds(i * step, step)
        held[rows, :] = dot(slot_grad[i * step : (i + 1) * step], onehot[...], (1, 0)).astype(BF16)
        copies.append(pltpu.make_async_copy(held.at[rows], out.at[rows], sems.at[i]))
        copies[i].start()
    for copy in copies:
        copy.wait()


def local(tokens, out_grad, slot_rows, expert_counts, route_prob, w_gate, w_up, w_down):
    fsdp, experts = lax.axis_size("fsdp"), lax.axis_size("expert")
    steps = fsdp.bit_length() - 1
    token_count, features = tokens.shape
    _, _, slots = slot_rows.shape
    rows = experts * slots
    hidden = w_gate.shape[2]
    half, quarter = hidden // 2, hidden // 4
    def swap(x, *bits):
        mask = sum(1 << b for b in bits)
        return lax.ppermute(x, "fsdp", [(i, i ^ mask) for i in range(fsdp)])

    def to_expert(x):
        if experts == 2:
            return x[0], lax.ppermute(x[1], "expert", [(0, 1), (1, 0)])[None]
        moved = lax.all_to_all(x, "expert", split_axis=0, concat_axis=0, tiled=True)
        return moved[0], moved[1:]

    half_shape = jax.ShapeDtypeStruct((3, features, half), BF16)
    rows_out, onehot, far_weights = pl.pallas_call(
        gather_kernel,
        out_shape=(
            jax.ShapeDtypeStruct((experts, 2, slots, features), BF16),
            jax.ShapeDtypeStruct((rows, token_count), BF16),
            half_shape,
        ),
        in_specs=[HBM] * 6,
        out_specs=(VMEM,) * 3,
        scratch_shapes=[
            pltpu.SMEM((experts, slots), jnp.int32),
            pltpu.VMEM((features, token_count), BF16),
            pltpu.VMEM((features, token_count), BF16),
            pltpu.VMEM((rows, token_count), F32),
            pltpu.SemaphoreType.DMA((3,)),
            pltpu.SemaphoreType.DMA((3,)),
        ],
        compiler_params=PARAMS,
        name="gather_rows",
    )(*(in_hbm(x) for x in (slot_rows[0], tokens.T, out_grad.T, w_gate, w_up, w_down)))
    own, recv = to_expert(rows_out)
    if experts == 2:
        crossed = [(f * 2 + x, (f ^ 1) * 2 + 1 - x) for f in range(fsdp) for x in range(2)]
        other_recv = lax.ppermute(rows_out[1], ("fsdp", "expert"), crossed)[None]
    else:
        other_recv = swap(recv, 0)
    other_own = swap(own, 0)
    other_weights = swap(far_weights, 0)
    near_weights = pl.pallas_call(
        load_kernel,
        out_shape=half_shape,
        in_specs=[VMEM] + [HBM] * 3,
        out_specs=VMEM,
        scratch_shapes=[pltpu.SemaphoreType.DMA((3,))],
        compiler_params=PARAMS,
        cost_estimate=pl.CostEstimate(flops=0, bytes_accessed=6 * features * half, transcendentals=0),
        name="load_weights",
    )(own, *(in_hbm(w) for w in (w_gate, w_up, w_down)))
    kept = pl.pallas_call(
        partial_kernel,
        out_shape=jax.ShapeDtypeStruct((4, 3 * rows // 2, quarter), F32),
        in_specs=[VMEM] * 3,
        out_specs=VMEM,
        compiler_params=PARAMS,
        cost_estimate=pl.CostEstimate(
            flops=6 * rows * features * half, bytes_accessed=6 * features * half, transcendentals=0
        ),
        name="partial_sums",
    )(own, recv, near_weights)
    turned_shape = jax.ShapeDtypeStruct((features, rows), BF16)
    fact_shape = jax.ShapeDtypeStruct((rows // 2, 128), F32)
    diagonal_shape = jax.ShapeDtypeStruct((rows // 2, (rows + 127) // 128 * 128), F32)
    tok_t, grad_t, scale, live, diagonal = pl.pallas_call(
        rows_kernel,
        out_shape=(turned_shape, turned_shape, fact_shape, fact_shape, diagonal_shape),
        in_specs=[SMEM] + [VMEM] * 3,
        out_specs=(VMEM,) * 5,
        compiler_params=PARAMS,
        cost_estimate=pl.CostEstimate(flops=0, bytes_accessed=8 * features * rows, transcendentals=0),
        name="row_facts",
    )(expert_counts[0], own, recv, route_prob)
    coded_shape = jax.ShapeDtypeStruct((3 * rows // 2 + 8, quarter), F32)
    total, power, *sent = pl.pallas_call(
        add_kernel,
        out_shape=(
            jax.ShapeDtypeStruct((3 * rows // 2, quarter), F32),
            jax.ShapeDtypeStruct((8, quarter), F32),
        )
        + (coded_shape,) * 3,
        in_specs=[VMEM] * 4,
        out_specs=(VMEM,) * 5,
        scratch_shapes=[pltpu.VMEM(kept.shape, F32)],
        compiler_params=PARAMS,
        name="add_other_core",
    )(kept, other_own, other_recv, other_weights)
    arrived = [swap(x.astype(F16), *bits) for x, bits in zip(sent, ((1,), (2,), (1, 2)))]
    for x in arrived:
        chunk, its_power = decoded(x)
        total, power = total + chunk, jnp.maximum(power, its_power)
    power += 2.0
    for b in range(3, steps):
        arrived, its_power = decoded(swap(coded(total, power).astype(F16), b))
        if b < steps - 1:
            total, power = total + arrived, jnp.maximum(power, its_power) + 1.0
    acts = pl.pallas_call(
        hidden_kernel,
        out_shape=jax.ShapeDtypeStruct((3 * rows // 2 + 8, quarter), BF16),
        in_specs=[VMEM] * 5,
        out_specs=VMEM,
        compiler_params=PARAMS,
        name="hidden",
    )(scale, live, diagonal, total, arrived)
    near = [acts, swap(acts, 1), swap(acts, 2), swap(acts, 1, 2)]
    far = swap(jnp.stack(near), 0)

    grad_shape = jax.ShapeDtypeStruct((1, features, hidden), F32)

    def held(count):
        return [pltpu.VMEM((count, features, quarter), F32), pltpu.SemaphoreType.DMA((count,))]

    near_slot, *grads = pl.pallas_call(
        near_kernel,
        out_shape=(jax.ShapeDtypeStruct((rows, features), F32),) + (grad_shape,) * 3,
        in_specs=[VMEM] * 7,
        out_specs=(VMEM,) + (HBM,) * 3,
        scratch_shapes=held(3),
        compiler_params=PARAMS,
        cost_estimate=pl.CostEstimate(
            flops=4 * rows * features * hidden, bytes_accessed=3 * features * hidden, transcendentals=0
        ),
        name="near_piece",
    )(*near, near_weights, tok_t, grad_t)
    slot_grad = pl.pallas_call(
        slot_kernel,
        out_shape=jax.ShapeDtypeStruct((experts, slots, features), BF16),
        in_specs=[VMEM] * 3,
        out_specs=VMEM,
        compiler_params=PARAMS,
        name="slot_grad",
    )(near_slot, far, far_weights)
    slot_own, slot_recv = to_expert(slot_grad)
    gate_grad, up_grad, down_grad, prob_grad = pl.pallas_call(
        weight_grad_kernel,
        out_shape=(grad_shape,) * 3 + (jax.ShapeDtypeStruct((1, rows // fsdp), F32),),
        in_specs=[VMEM] * 7 + [HBM] * 3,
        out_specs=(HBM,) * 4,
        scratch_shapes=held(9) + [pltpu.VMEM((1, rows // fsdp), F32), pltpu.SemaphoreType.DMA],
        input_output_aliases={7 + i: i for i in range(3)},
        compiler_params=PARAMS,
        cost_estimate=pl.CostEstimate(
            flops=4 * rows * features * hidden, bytes_accessed=9 * features * hidden, transcendentals=0
        ),
        name="weight_grads",
    )(*near, far, tok_t, grad_t, *grads)

    token_grad = pl.pallas_call(
        token_grad_kernel,
        out_shape=jax.ShapeDtypeStruct((features, token_count), BF16),
        in_specs=[VMEM] * 3,
        out_specs=HBM,
        scratch_shapes=[pltpu.VMEM((features, token_count), BF16), pltpu.SemaphoreType.DMA((5,))],
        compiler_params=PARAMS,
        name="token_grad",
    )(slot_own, slot_recv, onehot).T
    return (token_grad, gate_grad, up_grad, down_grad, prob_grad)


def solution(mesh):
    return jax.shard_map(
        local,
        mesh=mesh,
        in_specs=(
            P("expert", "fsdp"),
            P("expert", "fsdp"),
            P("expert", None, None),
            P("expert", None),
            P("expert", None),
            P("expert", "fsdp", None),
            P("expert", "fsdp", None),
            P("expert", "fsdp", None),
        ),
        out_specs=(
            P("expert", "fsdp"),
            P("expert", "fsdp", None),
            P("expert", "fsdp", None),
            P("expert", "fsdp", None),
            P("expert", "fsdp"),
        ),
        check_vma=False,
    )
```

```python
import functools

import jax
import jax.numpy as jnp
from jax import lax
from jax.experimental import pallas as pl
from jax.experimental.pallas import tpu as pltpu
from jax.sharding import PartitionSpec as P

BF16 = jnp.bfloat16
F32 = jnp.float32
F16 = jnp.float16
VMEM = pl.BlockSpec(memory_space=pltpu.VMEM)
HBM = pl.BlockSpec(memory_space=pltpu.HBM)
SMEM = pl.BlockSpec(memory_space=pltpu.SMEM)
PARAMS = pltpu.CompilerParams(vmem_limit_bytes=40 * 2**20)

def in_hbm(x):
    return pltpu.with_memory_space_constraint(x, pltpu.HBM)


def dot(a, b, contract):
    return lax.dot_general(a, b, ((contract[0:1], contract[1:2]), ((), ())), preferred_element_type=F32)


def place(side, jy, width):
    me = lax.axis_index("fsdp")
    half = (me & 1) ^ side
    return pl.multiple_of((half * 2 + (((me >> 1) & 1) ^ jy)) * width, 128)


def place_in_half(jy, width):
    return pl.multiple_of((((lax.axis_index("fsdp") >> 1) & 1) ^ jy) * width, 128)


def half_copies(side, weights, to, sems):
    width = to.shape[2]
    at = pl.ds(pl.multiple_of(((lax.axis_index("fsdp") & 1) ^ side) * width, 128), width)
    return [pltpu.make_async_copy(w.at[0, :, at], to.at[i], sems.at[i]) for i, w in enumerate(weights)]


def row_part():
    return (lax.axis_index("fsdp") >> 2) & 1


def first_expert(experts):
    return lax.axis_index("expert") if experts == 2 else 0


def gather_kernel(slot_rows_hbm, tokens_hbm, grads_hbm, *refs):
    weights, (rows_out, onehot_out, far_out, slot_rows, tokens_t, grads_t, onehot_f, sems, far_sems) = refs[:3], refs[3:]
    copies = [
        pltpu.make_async_copy(source, to, sems.at[i])
        for i, (source, to) in enumerate(((slot_rows_hbm, slot_rows), (tokens_hbm, tokens_t), (grads_hbm, grads_t)))
    ]
    far_copies = half_copies(1, weights, far_out, far_sems)
    for copy in copies + far_copies:
        copy.start()
    experts, slots = slot_rows.shape
    count = tokens_t.shape[1]
    first = first_expert(experts)
    lane = lax.broadcasted_iota(jnp.int32, (8, count), 1)
    sub = lax.broadcasted_iota(jnp.int32, (8, count), 0)
    copies[0].wait()
    for j in range(experts):
        expert = lax.rem(first + j, experts)
        for base in range(0, slots, 8):
            picked = jnp.zeros((8, count), jnp.int32)
            for r in range(8):
                picked = jnp.where(sub == r, slot_rows[expert, base + r], picked)
            onehot_f[pl.ds(j * slots + base, 8), :] = (picked == lane).astype(F32)
    onehot = onehot_f[...].astype(BF16)
    onehot_out[...] = onehot
    for kind, source in enumerate((tokens_t, grads_t)):
        copies[1 + kind].wait()
        rows = dot(onehot, source[...], (1, 1))
        for j in range(experts):
            rows_out[j, kind] = rows[j * slots : (j + 1) * slots].astype(BF16)
    for copy in far_copies:
        copy.wait()


def load_kernel(after, w_gate, w_up, w_down, out, sems):
    del after
    copies = half_copies(0, (w_gate, w_up, w_down), out, sems)
    for copy in copies:
        copy.start()
    for copy in copies:
        copy.wait()


def stacked_rows(own, recv, kind):
    blocks = [own[kind]] + [recv[j, kind] for j in range(recv.shape[0])]
    return jnp.concatenate([block.astype(F32) for block in blocks], axis=0)


def partial_sums(own, recv, weights, width, jy, q):
    rows = stacked_rows(own, recv, q // 2).astype(BF16)
    return dot(rows, weights[q, :, pl.ds(place_in_half(jy, width), width)], (1, 0))


def partial_kernel(own, recv, weights, out):
    chunk_rows, width = out.shape[1] // 3, out.shape[2]
    for jy in range(2):
        for q in range(3):
            sums = partial_sums(own, recv, weights, width, jy, q)
            for part in range(2):
                chunk = (row_part() ^ part) * 2 + jy
                out[chunk, pl.ds(q * chunk_rows, chunk_rows), :] = sums[part * chunk_rows : (part + 1) * chunk_rows]


def rows_kernel(counts, own, recv, prob, tok_t, grad_t, scale_out, live_out, diagonal_out):
    part0 = row_part()
    rows, lanes = diagonal_out.shape
    for to, x in ((tok_t, stacked_rows(own, recv, 0)), (grad_t, stacked_rows(own, recv, 1))):
        low, high = x[:rows], x[rows:]
        near, far = jnp.where(part0 == 0, low, high), jnp.where(part0 == 0, high, low)
        to[...] = jnp.concatenate([near, far], axis=0).T.astype(BF16)
    experts = counts.shape[0]
    slots = 2 * rows // experts
    first = first_expert(experts)
    row = lax.broadcasted_iota(jnp.int32, (rows, lanes), 0) + part0 * rows
    lane = lax.broadcasted_iota(jnp.int32, (rows, lanes), 1)
    slot, home, live_count = row, row, row
    for j in range(experts):
        source = lax.rem(first + j, experts)
        inside = (row >= j * slots) & (row < (j + 1) * slots)
        slot = jnp.where(inside, row - j * slots, slot)
        home = jnp.where(inside, source * slots + row - j * slots, home)
        live_count = jnp.where(inside, counts[source], live_count)
    live = (slot < live_count).astype(F32)
    diagonal = lane == home
    probs = jnp.concatenate([prob[...], jnp.zeros((1, lanes - 2 * rows), F32)], axis=1)
    row_prob = jnp.sum(jnp.where(diagonal, probs, 0.0), axis=1, keepdims=True)
    scale_out[...] = row_prob * live[:, :128]
    live_out[...] = live[:, :128]
    diagonal_out[...] = diagonal.astype(F32)


def add_kernel(kept, own, recv, weights, first, power_out, *refs):
    outs, summed = refs[:-1], refs[-1]
    partial_kernel(own, recv, weights, summed)
    rows = first.shape[0] // 3
    width = first.shape[1]
    chunks = [kept[j] + summed[j] for j in range(4)]
    first[...] = chunks[0]
    powers = []
    for q in range(3):
        most = functools.reduce(jnp.maximum, [jnp.abs(x[q * rows : (q + 1) * rows]) for x in chunks])
        most = jnp.maximum(jnp.max(most, axis=0, keepdims=True), 1e-30)
        powers.append(jnp.ceil(jnp.log2(most)) - 14.0)
    power_out[...] = jnp.concatenate(powers + [jnp.zeros((5, width), F32)], axis=0)
    for x, out in zip(chunks[1:], outs):
        for q in range(3):
            out[pl.ds(q * rows, rows), :] = x[q * rows : (q + 1) * rows] * jnp.exp2(-powers[q])
        out[pl.ds(3 * rows, 8), :] = power_out[...]


def scaled(x, power):
    rows = x.shape[0] // 3
    return (x.reshape(3, rows, -1) * jnp.exp2(power[:3])[:, None]).reshape(x.shape)


def coded(x, power):
    return jnp.concatenate([scaled(x, -power), power], axis=0)


def decoded(x):
    x = x.astype(F32)
    return scaled(x[:-8], x[-8:]), x[-8:]


def hidden_kernel(scale, live, diagonal, sums, recv, out):
    rows = sums.shape[0] // 3
    width = sums.shape[1]
    powers = [recv[pl.ds(3 * rows + q, 1), :] for q in range(3)]
    total = [
        sums[pl.ds(q * rows, rows), :] + recv[pl.ds(q * rows, rows), :] * jnp.exp2(power)
        for q, power in enumerate(powers)
    ]
    gate, up, down = total
    row_scale = jnp.concatenate([scale[...]] * (width // 128), axis=1)
    sigmoid = jax.nn.sigmoid(gate)
    silu = gate * sigmoid
    hidden = (silu * up).astype(BF16).astype(F32)
    hidden_grad = down * row_scale
    gate_act_grad = hidden_grad * up * sigmoid * (1.0 + gate * (1.0 - sigmoid))
    prob_grad = live[:, :1] * jnp.sum(hidden * down, axis=1, keepdims=True)
    prob_row = jnp.sum(diagonal[...] * prob_grad, axis=0, keepdims=True)
    high = prob_row.astype(BF16).astype(F32)
    tail = jnp.concatenate([high, prob_row - high, jnp.zeros((6, prob_row.shape[1]), F32)], axis=0)
    tail = jnp.concatenate([tail, jnp.zeros((8, width - prob_row.shape[1]), F32)], axis=1)
    out[...] = jnp.concatenate([hidden * row_scale, gate_act_grad, hidden_grad * silu, tail], axis=0).astype(BF16)


def parts(a, b):
    a, b = a[...].astype(F32), b[...].astype(F32)
    rows = (a.shape[0] - 8) // 3
    both = [jnp.concatenate([a[q * rows : (q + 1) * rows], b[q * rows : (q + 1) * rows]], axis=0) for q in range(3)]
    return [x.astype(BF16) for x in both]


def slot_part(a, b, weights, jy):
    _, gate_act_grad, up_act_grad = parts(a, b)
    at = pl.ds(place_in_half(jy, a.shape[1]), a.shape[1])
    return dot(gate_act_grad, weights[0, :, at], (1, 1)) + dot(up_act_grad, weights[1, :, at], (1, 1))


def weight_grad_copies(pieces, tok_t, grad_t, outs, held, sems):
    copies = []
    for a, b, column in pieces:
        down, gate, up = parts(a, b)
        for x, y, out in ((tok_t, gate, outs[0]), (tok_t, up, outs[1]), (grad_t, down, outs[2])):
            n = len(copies)
            held[n] = dot(x[...], y, (1, 0))
            copies.append(pltpu.make_async_copy(held.at[n], out.at[0, :, pl.ds(column, a.shape[1])], sems.at[n]))
            copies[n].start()
    return copies


def near_kernel(near0, near1, near2, near3, weights, tok_t, grad_t, out, gate_grad, up_grad, down_grad, held, sems):
    width = near0.shape[1]
    pieces = [(near0, near2, place(0, 0, width))]
    copies = weight_grad_copies(pieces, tok_t, grad_t, (gate_grad, up_grad, down_grad), held, sems)
    out[...] = slot_part(near0, near2, weights, 0) + slot_part(near1, near3, weights, 1)
    for copy in copies:
        copy.wait()


def slot_kernel(before, far, weights, out):
    experts, slots, _ = out.shape
    total = before[...]
    for jy in range(2):
        total += slot_part(far.at[jy], far.at[2 + jy], weights, jy)
    for part in range(2):
        for j in range(experts // 2):
            start = (part * (experts // 2) + j) * slots
            out[(row_part() ^ part) * (experts // 2) + j] = total[start : start + slots].astype(BF16)


def weight_grad_kernel(near0, near1, near2, near3, far, tok_t, grad_t, *refs):
    gate_grad, up_grad, down_grad, prob_out, held, sems, prob_held, prob_sem = refs[3:]
    width = far.shape[2]
    pieces = [(near1, near3, place(0, 1, width))]
    pieces += [(far.at[jy], far.at[2 + jy], place(1, jy, width)) for jy in range(2)]
    copies = weight_grad_copies(pieces, tok_t, grad_t, (gate_grad, up_grad, down_grad), held, sems)
    tail = jnp.zeros((8, width), F32)
    for chunk in (near0, near1, near2, near3, far.at[0], far.at[1], far.at[2], far.at[3]):
        tail += chunk[...].astype(F32)[-8:]
    prob = jnp.broadcast_to(tail[0:1] + tail[1:2], (8, width))
    share = prob_out.shape[1]
    shift = lax.rem(width - lax.axis_index("fsdp") * share, width)
    prob_held[...] = pltpu.roll(prob, shift, 1)[:1, :share]
    copies.append(pltpu.make_async_copy(prob_held, prob_out, prob_sem))
    copies[-1].start()
    for copy in copies:
        copy.wait()


def token_grad_kernel(own, recv, onehot, out, held, sems):
    blocks = [own[...]] + [recv[j] for j in range(recv.shape[0])]
    slot_grad = jnp.concatenate([block.astype(F32) for block in blocks], axis=0).T.astype(BF16)
    copies = []
    step = out.shape[0] // 5
    for i in range(5):
        rows = pl.ds(i * step, step)
        held[rows, :] = dot(slot_grad[i * step : (i + 1) * step], onehot[...], (1, 0)).astype(BF16)
        copies.append(pltpu.make_async_copy(held.at[rows], out.at[rows], sems.at[i]))
        copies[i].start()
    for copy in copies:
        copy.wait()


def local(tokens, out_grad, slot_rows, expert_counts, route_prob, w_gate, w_up, w_down):
    fsdp, experts = lax.axis_size("fsdp"), lax.axis_size("expert")
    steps = fsdp.bit_length() - 1
    token_count, features = tokens.shape
    _, _, slots = slot_rows.shape
    rows = experts * slots
    hidden = w_gate.shape[2]
    half, quarter = hidden // 2, hidden // 4
    def swap(x, *bits):
        mask = sum(1 << b for b in bits)
        return lax.ppermute(x, "fsdp", [(i, i ^ mask) for i in range(fsdp)])

    def to_expert(x):
        if experts == 2:
            return x[0], lax.ppermute(x[1], "expert", [(0, 1), (1, 0)])[None]
        moved = lax.all_to_all(x, "expert", split_axis=0, concat_axis=0, tiled=True)
        return moved[0], moved[1:]

    half_shape = jax.ShapeDtypeStruct((3, features, half), BF16)
    rows_out, onehot, far_weights = pl.pallas_call(
        gather_kernel,
        out_shape=(
            jax.ShapeDtypeStruct((experts, 2, slots, features), BF16),
            jax.ShapeDtypeStruct((rows, token_count), BF16),
            half_shape,
        ),
        in_specs=[HBM] * 6,
        out_specs=(VMEM,) * 3,
        scratch_shapes=[
            pltpu.SMEM((experts, slots), jnp.int32),
            pltpu.VMEM((features, token_count), BF16),
            pltpu.VMEM((features, token_count), BF16),
            pltpu.VMEM((rows, token_count), F32),
            pltpu.SemaphoreType.DMA((3,)),
            pltpu.SemaphoreType.DMA((3,)),
        ],
        compiler_params=PARAMS,
        name="gather_rows",
    )(*(in_hbm(x) for x in (slot_rows[0], tokens.T, out_grad.T, w_gate, w_up, w_down)))
    own, recv = to_expert(rows_out)
    if experts == 2:
        crossed = [(f * 2 + x, (f ^ 1) * 2 + 1 - x) for f in range(fsdp) for x in range(2)]
        other_recv = lax.ppermute(rows_out[1], ("fsdp", "expert"), crossed)[None]
    else:
        other_recv = swap(recv, 0)
    other_own = swap(own, 0)
    other_weights = swap(far_weights, 0)
    near_weights = pl.pallas_call(
        load_kernel,
        out_shape=half_shape,
        in_specs=[VMEM] + [HBM] * 3,
        out_specs=VMEM,
        scratch_shapes=[pltpu.SemaphoreType.DMA((3,))],
        compiler_params=PARAMS,
        cost_estimate=pl.CostEstimate(flops=0, bytes_accessed=6 * features * half, transcendentals=0),
        name="load_weights",
    )(own, *(in_hbm(w) for w in (w_gate, w_up, w_down)))
    kept = pl.pallas_call(
        partial_kernel,
        out_shape=jax.ShapeDtypeStruct((4, 3 * rows // 2, quarter), F32),
        in_specs=[VMEM] * 3,
        out_specs=VMEM,
        compiler_params=PARAMS,
        cost_estimate=pl.CostEstimate(
            flops=6 * rows * features * half, bytes_accessed=6 * features * half, transcendentals=0
        ),
        name="partial_sums",
    )(own, recv, near_weights)
    turned_shape = jax.ShapeDtypeStruct((features, rows), BF16)
    fact_shape = jax.ShapeDtypeStruct((rows // 2, 128), F32)
    diagonal_shape = jax.ShapeDtypeStruct((rows // 2, (rows + 127) // 128 * 128), F32)
    tok_t, grad_t, scale, live, diagonal = pl.pallas_call(
        rows_kernel,
        out_shape=(turned_shape, turned_shape, fact_shape, fact_shape, diagonal_shape),
        in_specs=[SMEM] + [VMEM] * 3,
        out_specs=(VMEM,) * 5,
        compiler_params=PARAMS,
        cost_estimate=pl.CostEstimate(flops=0, bytes_accessed=8 * features * rows, transcendentals=0),
        name="row_facts",
    )(expert_counts[0], own, recv, route_prob)
    coded_shape = jax.ShapeDtypeStruct((3 * rows // 2 + 8, quarter), F32)
    total, power, *sent = pl.pallas_call(
        add_kernel,
        out_shape=(
            jax.ShapeDtypeStruct((3 * rows // 2, quarter), F32),
            jax.ShapeDtypeStruct((8, quarter), F32),
        )
        + (coded_shape,) * 3,
        in_specs=[VMEM] * 4,
        out_specs=(VMEM,) * 5,
        scratch_shapes=[pltpu.VMEM(kept.shape, F32)],
        compiler_params=PARAMS,
        name="add_other_core",
    )(kept, other_own, other_recv, other_weights)
    arrived = [swap(x.astype(F16), *bits) for x, bits in zip(sent, ((1,), (2,), (1, 2)))]
    for x in arrived:
        chunk, its_power = decoded(x)
        total, power = total + chunk, jnp.maximum(power, its_power)
    power += 2.0
    for b in range(3, steps):
        arrived = swap(coded(total, power).astype(F16), b)
        if b < steps - 1:
            chunk, its_power = decoded(arrived)
            total, power = total + chunk, jnp.maximum(power, its_power) + 1.0
    acts = pl.pallas_call(
        hidden_kernel,
        out_shape=jax.ShapeDtypeStruct((3 * rows // 2 + 8, quarter), BF16),
        in_specs=[VMEM] * 5,
        out_specs=VMEM,
        compiler_params=PARAMS,
        name="hidden",
    )(scale, live, diagonal, total, arrived.astype(F32))
    near = [acts, swap(acts, 1), swap(acts, 2), swap(acts, 1, 2)]
    far = swap(jnp.stack(near), 0)

    grad_shape = jax.ShapeDtypeStruct((1, features, hidden), F32)

    def held(count):
        return [pltpu.VMEM((count, features, quarter), F32), pltpu.SemaphoreType.DMA((count,))]

    near_slot, *grads = pl.pallas_call(
        near_kernel,
        out_shape=(jax.ShapeDtypeStruct((rows, features), F32),) + (grad_shape,) * 3,
        in_specs=[VMEM] * 7,
        out_specs=(VMEM,) + (HBM,) * 3,
        scratch_shapes=held(3),
        compiler_params=PARAMS,
        cost_estimate=pl.CostEstimate(
            flops=4 * rows * features * hidden, bytes_accessed=3 * features * hidden, transcendentals=0
        ),
        name="near_piece",
    )(*near, near_weights, tok_t, grad_t)
    slot_grad = pl.pallas_call(
        slot_kernel,
        out_shape=jax.ShapeDtypeStruct((experts, slots, features), BF16),
        in_specs=[VMEM] * 3,
        out_specs=VMEM,
        compiler_params=PARAMS,
        name="slot_grad",
    )(near_slot, far, far_weights)
    slot_own, slot_recv = to_expert(slot_grad)
    gate_grad, up_grad, down_grad, prob_grad = pl.pallas_call(
        weight_grad_kernel,
        out_shape=(grad_shape,) * 3 + (jax.ShapeDtypeStruct((1, rows // fsdp), F32),),
        in_specs=[VMEM] * 7 + [HBM] * 3,
        out_specs=(HBM,) * 4,
        scratch_shapes=held(9) + [pltpu.VMEM((1, rows // fsdp), F32), pltpu.SemaphoreType.DMA],
        input_output_aliases={7 + i: i for i in range(3)},
        compiler_params=PARAMS,
        cost_estimate=pl.CostEstimate(
            flops=4 * rows * features * hidden, bytes_accessed=9 * features * hidden, transcendentals=0
        ),
        name="weight_grads",
    )(*near, far, tok_t, grad_t, *grads)

    token_grad = pl.pallas_call(
        token_grad_kernel,
        out_shape=jax.ShapeDtypeStruct((features, token_count), BF16),
        in_specs=[VMEM] * 3,
        out_specs=HBM,
        scratch_shapes=[pltpu.VMEM((features, token_count), BF16), pltpu.SemaphoreType.DMA((5,))],
        compiler_params=PARAMS,
        name="token_grad",
    )(slot_own, slot_recv, onehot).T
    return (token_grad, gate_grad, up_grad, down_grad, prob_grad)


def solution(mesh):
    return jax.shard_map(
        local,
        mesh=mesh,
        in_specs=(
            P("expert", "fsdp"),
            P("expert", "fsdp"),
            P("expert", None, None),
            P("expert", None),
            P("expert", None),
            P("expert", "fsdp", None),
            P("expert", "fsdp", None),
            P("expert", "fsdp", None),
        ),
        out_specs=(
            P("expert", "fsdp"),
            P("expert", "fsdp", None),
            P("expert", "fsdp", None),
            P("expert", "fsdp", None),
            P("expert", "fsdp"),
        ),
        check_vma=False,
    )
```
